256 devices in a mesh: nrow: 8 (over z), dcol: 32 (over y, x, core).
Axes of the slice: x: 4, y: 4, z: 8, core: 2. Of those that a mesh axis runs over, the one named last changes fastest.
Arguments:
- noise: float32 [4096, 4096], P('nrow', 'dcol'), may hold values from -15 to 15
- data: float32 [12288, 4096], P('dcol', 'nrow'), may hold values from -15 to 15
Outputs:
- noise_target: float32 [4096, 4096], P('nrow', 'dcol')
- data_target: float32 [12288, 4096], P('dcol', 'nrow')
The draws below stay inside these ranges and needn't reach their ends.
All inputs are finite; a program needn't handle non-finite values.
Results may differ from the reference program's by a relative error of at most 0.0003.
Values sent between devices are 32-bit elements; how exact they have to be, the bound alone decides.
No kernel may reach another device: no remote copies, remote signals or barrier semaphores. Data moves between devices by JAX's collectives and lax.ppermute only.
A program may use at most 64 MiB of HBM per device.

```python
import math
import jax
import jax.numpy as jnp
from jax import lax

D = 4096
ITERS = 3
N = 4096
M = 12288


def latent_rows(key, salt, rows):
    subkeys = jax.random.split(jax.random.fold_in(key, salt), 3)
    gauss = jnp.clip(jax.random.normal(subkeys[0], (rows, D), jnp.float32), -6.0, 6.0)
    values = gauss
    scales = jnp.exp(jax.random.uniform(subkeys[2], (rows, 1), jnp.float32, math.log(0.5), math.log(2.5)))
    return values * scales


def paired_data(key):
    base = latent_rows(key, 5, M)
    return base.at[16:32].set(base[16:32])


def draw_data(key, part):
    return paired_data(key)


def draw_noise(key, part):
    key = jax.random.fold_in(key, 9)
    return latent_rows(key, 3, N)


def setup_inputs(seed: int = 0) -> dict:
    key_list = jax.random.split(jax.random.key(seed), 3)
    return {
        "noise": draw_noise(jax.random.fold_in(key_list[2], 71), 0),
        "data": draw_data(jax.random.fold_in(key_list[2], 71), 0),
    }


EPSILON = 0.02


def max_lse(scores, axis):
    biggest = jnp.max(scores, axis=axis, keepdims=True)
    return jnp.squeeze(biggest, axis) + jnp.log(jnp.sum(jnp.exp(scores - biggest), axis=axis))


def shifted_lse(scores, shift, axis):
    return shift + jnp.log(jnp.sum(jnp.exp(scores - jnp.expand_dims(shift, axis)), axis=axis))


def reference(noise, data):
    precise = lax.Precision.HIGHEST
    noise_sq = jnp.sum(noise * noise, axis=1) / D
    data_sq = jnp.sum(data * data, axis=1) / D
    inner_prod = lax.dot_general(noise, data, (((1,), (1,)), ((), ())), precision=precise, preferred_element_type=jnp.float32)
    distance = noise_sq[:, None] + data_sq[None, :] - 2.0 * inner_prod / D
    log_noise = -math.log(N)
    log_data = -math.log(M)
    data_pot = jnp.zeros((M,), jnp.float32)
    noise_pot = jnp.zeros((N,), jnp.float32)
    for sweep in range(ITERS):
        row_scores = (data_pot[None, :] - distance) / EPSILON
        if sweep == 0:
            row_value = max_lse(row_scores, 1)
        else:
            row_value = shifted_lse(row_scores, log_noise - noise_pot / EPSILON, 1)
        noise_pot = EPSILON * log_noise - EPSILON * row_value
        col_scores = (noise_pot[:, None] - distance) / EPSILON
        if sweep == 0:
            col_value = max_lse(col_scores, 0)
        else:
            col_value = shifted_lse(col_scores, log_data - data_pot / EPSILON, 0)
        data_pot = EPSILON * log_data - EPSILON * col_value
    row_scores = (data_pot[None, :] - distance) / EPSILON
    row_value = shifted_lse(row_scores, log_noise - noise_pot / EPSILON, 1)
    row_weight = jnp.exp(row_scores - row_value[:, None])
    noise_target = jnp.dot(row_weight, data, precision=precise, preferred_element_type=jnp.float32)
    col_lse = log_data - data_pot / EPSILON
    col_weight = jnp.exp((noise_pot[:, None] - distance) / EPSILON - col_lse[None, :])
    data_target = lax.dot_general(col_weight, noise, (((0,), (0,)), ((), ())), precision=precise, preferred_element_type=jnp.float32)
    return noise_target, data_target
```

```python
import functools
import math

import jax
import jax.numpy as jnp
from jax import lax
from jax.experimental import pallas as pl
from jax.experimental.pallas import tpu as pltpu
from jax.sharding import Mesh, PartitionSpec as P

ITERS = 3
EPSILON = 0.02
VMEM_LIMIT = 56 * 1024 * 1024
BF16 = jnp.bfloat16
F32 = jnp.float32


def shift(v, axis, k):
    n = lax.axis_size(axis)
    return lax.ppermute(v, axis, [(i, (i + k) % n) for i in range(n)])


def swap(v, axis, k):
    n = lax.axis_size(axis)
    return lax.ppermute(v, axis, [(i, i ^ k) for i in range(n)])


def split(v):
    hi = v.astype(BF16)
    return hi, (v - hi.astype(F32)).astype(BF16)


def dot3(ah, al, bh, bl, dims):
    dot = functools.partial(
        lax.dot_general, dimension_numbers=(dims, ((), ())), preferred_element_type=F32
    )
    return dot(ah, bh) + (dot(ah, bl) + dot(al, bh))


def others(v, axis):
    return [shift(v, axis, k) for k in (1, 2, 3)]


def gather_order(me, slot):
    return lax.rem(me - slot + 4, 4)


def prep_kernel(pos, a, ao, b, bo, hi, lo, sq, share):
    core, row, first = pos[0], pos[3], pos[4]

    def place(own, oth):
        zero = core == 0
        return jnp.concatenate(
            [jnp.where(zero, own, oth), jnp.where(zero, oth, own)], axis=1
        )

    full = jnp.concatenate([place(a[0], ao[0]), place(b[0], bo[0])], axis=0)
    h, l = split(full)
    hi[...] = h
    lo[...] = l
    squares = full * full

    @pl.when(pl.program_id(0) == 0)
    def _():
        sq[...] = jnp.zeros_like(sq)

    sq[...] += squares[:, :128] + squares[:, 128:]
    rows = pl.ds(pl.multiple_of(row, 16), 16)
    top = place(a[0, rows, :], ao[0, rows, :])
    low = place(b[0, rows, :], bo[0, rows, :])
    share[...] = jnp.where(first == 1, top, low)


def prep(pos, a, ao, b, bo):
    half = a.shape[1]

    def block(g, p):
        y = gather_order(p[2], g // 4)
        x = gather_order(p[1], g % 4)
        return (0, y * 4 + x)

    spec_a = pl.BlockSpec((1, half, 128), lambda g, p: (g, 0, 0))
    spec_b = pl.BlockSpec((1, half, 128), lambda g, p: ((g % 4) * 4 + g // 4, 0, 0))
    return pl.pallas_call(
        prep_kernel,
        grid_spec=pltpu.PrefetchScalarGridSpec(
            num_scalar_prefetch=1,
            grid=(16,),
            in_specs=[spec_a, spec_a, spec_b, spec_b],
            out_specs=[
                pl.BlockSpec((2 * half, 256), block),
                pl.BlockSpec((2 * half, 256), block),
                pl.BlockSpec((2 * half, 128), lambda g, p: (0, 0)),
                pl.BlockSpec((16, 256), block),
            ],
        ),
        out_shape=[
            jax.ShapeDtypeStruct((2 * half, 4096), BF16),
            jax.ShapeDtypeStruct((2 * half, 4096), BF16),
            jax.ShapeDtypeStruct((2 * half, 128), F32),
            jax.ShapeDtypeStruct((16, 4096), F32),
        ],
        compiler_params=pltpu.CompilerParams(vmem_limit_bytes=VMEM_LIMIT),
        cost_estimate=pl.CostEstimate(
            flops=4 * 512 * 4096, bytes_accessed=17 * 2**20, transcendentals=0
        ),
        name="noise_columns",
    )(pos, a, ao, b, bo)


def lane_sums(v):
    return v[:, :128] + v[:, 128:256] + v[:, 256:384] + v[:, 384:]


def inner_kernel(offsets, pos, nh, nl, *refs):
    count = len(offsets)
    pieces, (acc, dh, dl, sq) = refs[:count], refs[count:]
    z = pos[5]
    for k, offset in enumerate(offsets):
        cols = pl.ds(pl.multiple_of(lax.rem(z + offset, 8) * 512, 512), 512)
        piece = pieces[k][...]
        h, l = split(piece)
        dh[:, cols] = h
        dl[:, cols] = l
        part = dot3(h, l, nh[:, cols], nl[:, cols], ((1,), (1,)))
        square = lane_sums(piece * piece)
        if k == 0:
            acc[...] = part
            sq[...] = square
        else:
            acc[...] += part
            sq[...] += square


def whole():
    return pl.BlockSpec(memory_space=pltpu.VMEM)


def inner(offsets, pos, nh, nl, pieces):
    rows = pieces[0].shape[0]
    cols = nh.shape[0]
    return pl.pallas_call(
        functools.partial(inner_kernel, offsets),
        in_specs=[pl.BlockSpec(memory_space=pltpu.SMEM)] + [whole()] * (2 + len(pieces)),
        out_specs=[whole()] * 4,
        out_shape=[
            jax.ShapeDtypeStruct((rows, cols), F32),
            jax.ShapeDtypeStruct((rows, 4096), BF16),
            jax.ShapeDtypeStruct((rows, 4096), BF16),
            jax.ShapeDtypeStruct((rows, 128), F32),
        ],
        compiler_params=pltpu.CompilerParams(vmem_limit_bytes=VMEM_LIMIT),
        cost_estimate=pl.CostEstimate(
            flops=6 * 512 * 384 * 512 * len(pieces),
            bytes_accessed=20 * 2**20,
            transcendentals=0,
        ),
        name="inner_products",
    )(pos, nh, nl, *pieces)


def last_kernel(pos, nh, nl, top, low, acc, sq, nsq, dist, lh, ll):
    half = top.shape[0]
    cols = pl.ds(pl.multiple_of(lax.rem(pos[5] + 4, 8) * 512, 512), 512)
    for k, ref in enumerate((top, low)):
        rows = slice(k * half, (k + 1) * half)
        piece = ref[...]
        h, l = split(piece)
        lh[rows, :] = h
        ll[rows, :] = l
        part = acc[rows, :] + dot3(h, l, nh[:, cols], nl[:, cols], ((1,), (1,)))
        dsq = jnp.sum(sq[rows, :] + lane_sums(piece * piece), axis=1, keepdims=True)
        dist[rows, :] = nsq[...] + dsq * (1.0 / 4096) - part * (2.0 / 4096)


def last(pos, nh, nl, top, low, acc, sq, nsq):
    rows, cols = acc.shape
    return pl.pallas_call(
        last_kernel,
        in_specs=[pl.BlockSpec(memory_space=pltpu.SMEM)] + [whole()] * 7,
        out_specs=[whole()] * 3,
        out_shape=[
            jax.ShapeDtypeStruct((rows, cols), F32),
            jax.ShapeDtypeStruct((rows, 512), BF16),
            jax.ShapeDtypeStruct((rows, 512), BF16),
        ],
        compiler_params=pltpu.CompilerParams(vmem_limit_bytes=VMEM_LIMIT),
        cost_estimate=pl.CostEstimate(
            flops=6 * 512 * 384 * 512, bytes_accessed=8 * 2**20, transcendentals=0
        ),
        name="distance",
    )(pos, nh, nl, top, low, acc, sq, nsq)


def noise_part_kernel(pos, w, dh, dl, lh, ll, own, oth, wh, wl):
    core, z = pos[0], pos[5]

    @pl.when(pl.program_id(0) == 0)
    def _():
        h, l = split(w[...])
        wh[...] = h
        wl[...] = l

    is_last = pl.program_id(0) // 2 == lax.rem(z + 4, 8)
    h = jnp.where(is_last, lh[...], dh[...])
    l = jnp.where(is_last, ll[...], dl[...])
    res = dot3(wh[...], wl[...], h, l, ((1,), (0,)))
    left, right = res[:, :128], res[:, 128:]
    own[0] = jnp.where(core == 0, left, right)
    oth[0] = jnp.where(core == 0, right, left)


def noise_part(pos, w, dh, dl, lh, ll):
    rows, depth = w.shape

    def slot(g, p):
        y = lax.rem(g // 4 - p[2] + 4, 4)
        x = lax.rem(g % 4 - p[1] + 4, 4)
        return (y * 4 + x, 0, 0)

    data = pl.BlockSpec((depth, 256), lambda g, p: (0, g))
    tail = pl.BlockSpec((depth, 256), lambda g, p: (0, g % 2))
    return pl.pallas_call(
        noise_part_kernel,
        grid_spec=pltpu.PrefetchScalarGridSpec(
            num_scalar_prefetch=1,
            grid=(16,),
            in_specs=[
                pl.BlockSpec((rows, depth), lambda g, p: (0, 0)),
                data,
                data,
                tail,
                tail,
            ],
            out_specs=[pl.BlockSpec((1, rows, 128), slot)] * 2,
            scratch_shapes=[pltpu.VMEM((rows, depth), BF16)] * 2,
        ),
        out_shape=[jax.ShapeDtypeStruct((16, rows, 128), F32)] * 2,
        compiler_params=pltpu.CompilerParams(vmem_limit_bytes=VMEM_LIMIT),
        cost_estimate=pl.CostEstimate(
            flops=6 * 512 * 384 * 4096, bytes_accessed=16 * 2**20, transcendentals=0
        ),
        name="noise_part",
    )(pos, w, dh, dl, lh, ll)


def data_target_kernel(pos, dist, pot, norm, noise, out):
    score = (pot[0] - dist[0]) / EPSILON - norm[...]
    wh, wl = split(jnp.exp(score))
    n = noise[:, 0]
    nh, nl = split(n.reshape(n.shape[0] * n.shape[1], n.shape[2]))
    part = dot3(wh, wl, nh, nl, ((1,), (0,)))

    @pl.when(pl.program_id(0) == 0)
    def _():
        out[...] = part

    @pl.when(pl.program_id(0) > 0)
    def _():
        out[...] += part


def data_target_of(pos, dist, pot, norm, noise):
    _, rows, depth = dist.shape
    return pl.pallas_call(
        data_target_kernel,
        grid_spec=pltpu.PrefetchScalarGridSpec(
            num_scalar_prefetch=1,
            grid=(8,),
            in_specs=[
                pl.BlockSpec((1, rows, depth), lambda g, p: (g, 0, 0)),
                pl.BlockSpec((1, 1, depth), lambda g, p: (g ^ p[5], 0, 0)),
                pl.BlockSpec((rows, 1), lambda g, p: (0, 0)),
                pl.BlockSpec((32, 1, 16, 512), lambda g, p: (0, g, 0, 0)),
            ],
            out_specs=pl.BlockSpec((rows, 512), lambda g, p: (0, 0)),
        ),
        out_shape=jax.ShapeDtypeStruct((rows, 512), F32),
        compiler_params=pltpu.CompilerParams(vmem_limit_bytes=VMEM_LIMIT),
        cost_estimate=pl.CostEstimate(
            flops=6 * 512 * 384 * 4096,
            bytes_accessed=16 * 2**20,
            transcendentals=384 * 4096,
        ),
        name="data_target",
    )(pos, dist, pot, norm, noise)


def merge(parts):
    top = functools.reduce(jnp.maximum, [p[0] for p in parts])
    total = sum(p[1] * jnp.exp(p[0] - top) for p in parts)
    return jnp.stack([top, total])


def add(parts):
    return sum(parts)


def row_total(v, join):
    v = join([v, swap(v, "c", 1)])
    v = join([v] + others(v, "x"))
    return join([v] + others(v, "y"))


def col_total(v, join):
    v = join([v] + [swap(v, "z", k) for k in (1, 2, 3)])
    return join([v, swap(v, "z", 4)])


def on_device(noise, data):
    half = noise.shape[0] // 2
    rows = data.shape[0]
    total_noise = noise.shape[0] * lax.axis_size("z")
    total_data = rows * 32
    log_noise = -math.log(total_noise)
    log_data = -math.log(total_data)
    c, x, y, z = (lax.axis_index(a).astype(jnp.int32) for a in "cxyz")
    share_index = y * 8 + x * 2 + c
    pos = jnp.stack(
        [
            c,
            x,
            y,
            lax.rem(share_index, 16) * 16,
            (share_index < 16).astype(jnp.int32),
            z,
        ]
    )
    barrier = lax.optimization_barrier

    up, down = shift(data, "z", 1), shift(data, "z", -1)
    top, low = noise[:half], noise[half:]
    top_all = jnp.stack([top] + others(top, "x"))
    low_all = jnp.stack([low] + others(low, "y"))
    pieces = [(0, data), (7, up), (1, down)]
    up, down, top_all, low_all = barrier((up, down, top_all, low_all))
    up, down = shift(up, "z", 1), shift(down, "z", -1)
    pieces += [(6, up), (2, down)]
    top_full = jnp.concatenate([top_all] + others(top_all, "y"))
    low_full = jnp.concatenate([low_all] + others(low_all, "x"))
    up, down, top_full, low_full = barrier((up, down, top_full, low_full))
    up, down = shift(up, "z", 1), shift(down, "z", -1)
    pieces += [(5, up), (3, down)]
    top_other, low_other = swap(top_full, "c", 1), swap(low_full, "c", 1)
    nh, nl, nsq, share = prep(pos, top_full, top_other, low_full, low_other)
    up = shift(up[: rows // 2], "z", 1)
    down = shift(down[rows // 2 :], "z", -1)
    acc, dh, dl, dsq = inner(
        [k for k, _ in pieces], pos, nh, nl, [p for _, p in pieces]
    )
    nsq = (jnp.sum(nsq, axis=1) / 4096)[None, :]
    dist, lh, ll = last(pos, nh, nl, up, down, acc, dsq, nsq)

    share = share.reshape(16, 8, 512).transpose(1, 0, 2)
    noise_cols = lax.all_gather(
        lax.all_to_all(share, "z", 0, 0), ("y", "x", "c"), axis=0
    )
    dist_all = lax.all_gather(dist, "z", axis=0)
    dist_t = dist.T

    data_pot = jnp.zeros((rows,), F32)
    noise_pot = jnp.zeros((2 * half,), F32)
    for sweep in range(ITERS):
        scores = (data_pot[:, None] - dist) / EPSILON
        if sweep == 0:
            top = jnp.max(scores, axis=0)
            total = jnp.sum(jnp.exp(scores - top[None, :]), axis=0)
            top, total = row_total(jnp.stack([top, total]), merge)
        else:
            top = log_noise - noise_pot / EPSILON
            total = row_total(jnp.sum(jnp.exp(scores - top[None, :]), axis=0), add)
        noise_pot = EPSILON * log_noise - EPSILON * (top + jnp.log(total))
        scores = (noise_pot[None, :] - dist) / EPSILON
        if sweep == 0:
            top = jnp.max(scores, axis=1)
            total = jnp.sum(jnp.exp(scores - top[:, None]), axis=1)
            top, total = col_total(jnp.stack([top, total]), merge)
        else:
            top = log_data - data_pot / EPSILON
            total = jnp.sum(jnp.exp(scores - top[:, None]), axis=1)
            if sweep < ITERS - 1:
                total = col_total(total, add)
            else:
                both = [jnp.concatenate([total, noise_pot])]
                both += [swap(both[0], "z", k) for k in (1, 2, 3)]
                total = add([b[:rows] for b in both])
                both = jnp.concatenate([total] + [b[rows:] for b in both])
                far = swap(both, "z", 4)
                total = both[:rows] + far[:rows]
                pot_all = jnp.concatenate([both[rows:], far[rows:]])
        data_pot = EPSILON * log_data - EPSILON * (top + jnp.log(total))

    top = log_noise - noise_pot / EPSILON
    weight = jnp.exp((data_pot[None, :] - dist_t) / EPSILON - top[:, None])
    own, oth = noise_part(pos, weight, dh, dl, lh, ll)
    own = (own + swap(oth, "c", 1)).reshape(4, 4, 2 * half, 128)
    row_sum = row_total(jnp.sum(weight, axis=1), add)
    top, low = own[:, :, :half], own[:, :, half:]
    top = top[:, 0] + sum(shift(top[:, k], "x", k) for k in (1, 2, 3))
    low = low[0] + sum(shift(low[k], "y", k) for k in (1, 2, 3))
    top = top[0] + sum(shift(top[k], "y", k) for k in (1, 2, 3))
    low = low[0] + sum(shift(low[k], "x", k) for k in (1, 2, 3))
    noise_target = jnp.concatenate([top, low]) / row_sum[:, None]

    norm = (log_data - data_pot / EPSILON)[:, None]
    data_target = data_target_of(
        pos, dist_all, pot_all.reshape(8, 1, 2 * half), norm, noise_cols
    )
    return (noise_target, data_target)


def solution(mesh):
    devices = mesh.devices.reshape(8, 4, 4, 2)
    torus = Mesh(devices, ("z", "y", "x", "c"))
    plane = ("y", "x", "c")
    return jax.shard_map(
        on_device,
        mesh=torus,
        in_specs=(P("z", plane), P(plane, "z")),
        out_specs=(P("z", plane), P(plane, "z")),
        check_vma=False,
    )
```

```python
import functools
import math

import jax
import jax.numpy as jnp
from jax import lax
from jax.experimental import pallas as pl
from jax.experimental.pallas import tpu as pltpu
from jax.sharding import Mesh, PartitionSpec as P

ITERS = 3
EPSILON = 0.02
VMEM_LIMIT = 56 * 1024 * 1024
BF16 = jnp.bfloat16
F32 = jnp.float32


def shift(v, axis, k):
    n = lax.axis_size(axis)
    return lax.ppermute(v, axis, [(i, (i + k) % n) for i in range(n)])


def swap(v, axis, k):
    n = lax.axis_size(axis)
    return lax.ppermute(v, axis, [(i, i ^ k) for i in range(n)])


def split(v):
    hi = v.astype(BF16)
    return hi, (v - hi.astype(F32)).astype(BF16)


def anywhere():
    return pl.BlockSpec(memory_space=pl.ANY)


def in_vmem():
    return pl.BlockSpec(memory_space=pltpu.VMEM)


def in_smem():
    return pl.BlockSpec(memory_space=pltpu.SMEM)


def params():
    return pltpu.CompilerParams(vmem_limit_bytes=VMEM_LIMIT)


def dot3(a, b, a_dim, b_dim):
    ah, al = split(a)
    bh, bl = split(b)
    return lax.dot_general(
        jnp.concatenate([ah, ah, al], axis=a_dim),
        jnp.concatenate([bh, bl, bh], axis=b_dim),
        (((a_dim,), (b_dim,)), ((), ())),
        preferred_element_type=F32,
    )


def lane_sums(v):
    return v[:, :128] + v[:, 128:256] + v[:, 256:384] + v[:, 384:]


def each(count, step):
    lax.fori_loop(0, count, lambda k, _: (step(k), 0)[1], 0)


OFFSETS = (0, 7, 1, 6, 2, 5, 3, 4)


def chunk_of(z, k):
    m = (k + 1) // 2
    return lax.rem(z + jnp.where(lax.rem(k, 2) == 0, m, 8 - m), 8)


def columns(z):
    return pl.ds(pl.multiple_of(z * 512, 512), 512)


def inner_kernel(pos, noise, *refs):
    pieces = refs[:7]
    acc, dsq, nsq, nbuf, dbuf, nsem, dsem = refs[7:]

    def fetch_noise(k):
        return pltpu.make_async_copy(
            noise.at[:, columns(chunk_of(pos[3], k))], nbuf.at[k], nsem.at[k]
        )

    def fetch_data(k, ref):
        return pltpu.make_async_copy(ref, dbuf.at[k], dsem.at[k])

    for k, ref in enumerate(pieces):
        fetch_noise(k).start()
        fetch_data(k, ref).start()
    fetch_noise(7).start()
    acc[...] = jnp.zeros_like(acc)
    dsq[...] = jnp.zeros_like(dsq)
    nsq[...] = jnp.zeros_like(nsq)

    def step(k):
        fetch_noise(k).wait()
        fetch_data(k, pieces[0]).wait()
        n, d = nbuf[k], dbuf[k]
        acc[...] += dot3(d, n, 1, 1)
        dsq[...] += lane_sums(d * d)
        nsq[...] += lane_sums(n * n)

    each(7, step)
    fetch_noise(7).wait()
    n = nbuf[7]
    nsq[...] += lane_sums(n * n)


def inner(pos, noise, pieces):
    cols, rows = noise.shape[0], pieces[0].shape[0]
    return pl.pallas_call(
        inner_kernel,
        in_specs=[in_smem()] + [anywhere()] * 8,
        out_specs=[in_vmem()] * 3,
        out_shape=[
            jax.ShapeDtypeStruct((rows, cols), F32),
            jax.ShapeDtypeStruct((rows, 128), F32),
            jax.ShapeDtypeStruct((cols, 128), F32),
        ],
        scratch_shapes=[
            pltpu.VMEM((8, cols, 512), F32),
            pltpu.VMEM((7, rows, 512), F32),
            pltpu.SemaphoreType.DMA((8,)),
            pltpu.SemaphoreType.DMA((7,)),
        ],
        compiler_params=params(),
        cost_estimate=pl.CostEstimate(
            flops=6 * cols * rows * 3584, bytes_accessed=15 * 2**20, transcendentals=0
        ),
        name="inner_products",
    )(pos, noise, *pieces)


def distance_kernel(pos, noise, top, low, acc, dsq, nsq, dist, nbuf, dbuf, sems):
    half = top.shape[0]
    copies = [
        pltpu.make_async_copy(top, dbuf.at[:half], sems.at[0]),
        pltpu.make_async_copy(low, dbuf.at[half:], sems.at[1]),
        pltpu.make_async_copy(
            noise.at[:, columns(lax.rem(pos[3] + 4, 8))], nbuf, sems.at[2]
        ),
    ]
    for copy in copies:
        copy.start()
    for copy in copies:
        copy.wait()
    d = dbuf[...]
    inner_prod = acc[...] + dot3(d, nbuf[...], 1, 1)
    data_sq = jnp.sum(dsq[...] + lane_sums(d * d), axis=1, keepdims=True)
    dist[...] = nsq[...] + data_sq * (1.0 / 4096) - inner_prod * (2.0 / 4096)


def distance(pos, noise, top, low, acc, dsq, nsq):
    rows, cols = acc.shape
    return pl.pallas_call(
        distance_kernel,
        in_specs=[in_smem()] + [anywhere()] * 3 + [in_vmem()] * 3,
        out_specs=in_vmem(),
        out_shape=jax.ShapeDtypeStruct((rows, cols), F32),
        scratch_shapes=[
            pltpu.VMEM((cols, 512), F32),
            pltpu.VMEM((rows, 512), F32),
            pltpu.SemaphoreType.DMA((3,)),
        ],
        compiler_params=params(),
        cost_estimate=pl.CostEstimate(
            flops=6 * cols * rows * 512, bytes_accessed=4 * 2**20, transcendentals=0
        ),
        name="distance",
    )(pos, noise, top, low, acc, dsq, nsq)


def noise_part_kernel(pos, w, *refs):
    pieces = refs[:9]
    outs, (wcat, dbuf, obuf, dsem, osem) = refs[9:13], refs[13:]
    core, x, y, z = pos[0], pos[1], pos[2], pos[3]
    rows, depth = w.shape
    half, part = rows // 2, depth // 2
    sums = []
    for k, ref in enumerate(pieces):
        if k < 7:
            at = dbuf.at[lax.rem(z + OFFSETS[k], 8)]
        else:
            at = dbuf.at[lax.rem(z + 4, 8), (k - 7) * part : (k - 6) * part]
        sums.append(pltpu.make_async_copy(ref, at, dsem.at[k]))
    for copy in sums:
        copy.start()
    h, l = split(w[...])
    wcat[:, :depth] = h
    wcat[:, depth : 2 * depth] = h
    wcat[:, 2 * depth :] = l
    for copy in sums:
        copy.wait()

    def stores(g):
        dy = lax.rem(g // 4 - y + 4, 4)
        dx = lax.rem(lax.rem(g, 4) - x + 4, 4)
        slots = (dx * 4 + dy, dy * 4 + dx)
        copies = []
        for side in range(2):
            which = core if side == 0 else 1 - core
            for k in range(2):
                copies.append(
                    pltpu.make_async_copy(
                        obuf.at[which, g, pl.ds(k * half, half)],
                        outs[2 * side + k].at[slots[k]],
                        osem.at[2 * side + k, g],
                    )
                )
        return copies

    def step(k):
        h, l = split(dbuf[k])
        res = lax.dot_general(
            wcat[...],
            jnp.concatenate([h, l, h], axis=0),
            (((1,), (0,)), ((), ())),
            preferred_element_type=F32,
        )
        for j in range(2):
            obuf[0, 2 * k + j] = res[:, j * 256 : j * 256 + 128]
            obuf[1, 2 * k + j] = res[:, j * 256 + 128 : j * 256 + 256]
            for copy in stores(2 * k + j):
                copy.start()

    each(8, step)

    def finish(g):
        for copy in stores(g):
            copy.wait()

    each(16, finish)


def noise_part(pos, w, pieces):
    rows, depth = w.shape
    return pl.pallas_call(
        noise_part_kernel,
        in_specs=[in_smem(), in_vmem()] + [anywhere()] * 9,
        out_specs=[anywhere()] * 4,
        out_shape=[jax.ShapeDtypeStruct((16, rows // 2, 128), F32)] * 4,
        scratch_shapes=[
            pltpu.VMEM((rows, 3 * depth), BF16),
            pltpu.VMEM((8, depth, 512), F32),
            pltpu.VMEM((2, 16, rows, 128), F32),
            pltpu.SemaphoreType.DMA((9,)),
            pltpu.SemaphoreType.DMA((4, 16)),
        ],
        compiler_params=params(),
        cost_estimate=pl.CostEstimate(
            flops=6 * rows * depth * 4096, bytes_accessed=15 * 2**20, transcendentals=0
        ),
        name="noise_part",
    )(pos, w, *pieces)


def data_target_kernel(pos, dist, pot, norm, noise, out, dbuf, nbuf, dsem, nsem):
    def fetch(k):
        return (
            pltpu.make_async_copy(dist.at[k], dbuf.at[k], dsem.at[k]),
            pltpu.make_async_copy(noise.at[:, k], nbuf.at[k], nsem.at[k]),
        )

    def start(k):
        for copy in fetch(k):
            copy.start()

    each(8, start)
    out[...] = jnp.zeros_like(out)

    def step(k):
        for copy in fetch(k):
            copy.wait()
        own = pot[jnp.bitwise_xor(k, pos[3])]
        w = jnp.exp((own - dbuf[k]) / EPSILON - norm[...])
        n = nbuf[k]
        out[...] += dot3(w, n.reshape(n.shape[0] * n.shape[1], n.shape[2]), 1, 0)

    each(8, step)


def data_target_of(pos, dist, pot, norm, noise):
    _, rows, depth = dist.shape
    shares, _, share, width = noise.shape
    return pl.pallas_call(
        data_target_kernel,
        in_specs=[in_smem(), anywhere(), in_vmem(), in_vmem(), anywhere()],
        out_specs=in_vmem(),
        out_shape=jax.ShapeDtypeStruct((rows, width), F32),
        scratch_shapes=[
            pltpu.VMEM((8, rows, depth), F32),
            pltpu.VMEM((8, shares, share, width), F32),
            pltpu.SemaphoreType.DMA((8,)),
            pltpu.SemaphoreType.DMA((8,)),
        ],
        compiler_params=params(),
        cost_estimate=pl.CostEstimate(
            flops=6 * rows * depth * 8 * width,
            bytes_accessed=15 * 2**20,
            transcendentals=8 * rows * depth,
        ),
        name="data_target",
    )(pos, dist, pot, norm, noise)


def others(v, axis):
    return [shift(v, axis, k) for k in (1, 2, 3)]


def merge(parts):
    top = functools.reduce(jnp.maximum, [p[0] for p in parts])
    total = sum(p[1] * jnp.exp(p[0] - top) for p in parts)
    return jnp.stack([top, total])


def add(parts):
    return sum(parts)


def row_total(v, join):
    v = join([v, swap(v, "c", 1)])
    v = join([v] + others(v, "x"))
    return join([v] + others(v, "y"))


def col_total(v, join):
    v = join([v] + [swap(v, "z", k) for k in (1, 2, 3)])
    return join([v, swap(v, "z", 4)])


def scatter_sum(chunks, axis):
    n = chunks[2].shape[0] // 2
    up = shift(chunks[2][:n], axis, 1)
    down = shift(chunks[2][n:], axis, -1)
    up = jnp.concatenate([chunks[1][:n] + up, chunks[1][n:]])
    down = jnp.concatenate([chunks[3][:n], chunks[3][n:] + down])
    return chunks[0] + shift(up, axis, 1) + shift(down, axis, -1)


def on_device(noise, data):
    cols, rows = noise.shape[0], data.shape[0]
    log_noise = -math.log(cols * lax.axis_size("z"))
    log_data = -math.log(rows * 32)
    pos = jnp.stack([lax.axis_index(a).astype(jnp.int32) for a in ("c", "x", "y", "z")])
    barrier = lax.optimization_barrier
    plane = ("y", "x", "c")

    noise_full = lax.all_gather(noise, plane, axis=1, tiled=True)
    half = rows // 2
    up, down = shift(data, "z", 1), shift(data, "z", -1)
    share = noise.reshape(4, 4, 2, cols // 32, 128)
    share = lax.all_to_all(share, "c", 2, 3)
    share = lax.all_to_all(share, "x", 1, 2)
    up, down, share = barrier((up, down, share))
    pieces = [data, up, down]
    up, down = shift(up, "z", 1), shift(down, "z", -1)
    share = lax.all_to_all(share, "y", 0, 1).reshape(cols // 32, 8, 512)
    up, down, share = barrier((up, down, share))
    pieces += [up, down]
    up, down = shift(up, "z", 1), shift(down, "z", -1)
    share = lax.all_to_all(share, "z", 1, 0)
    up, down, share = barrier((up, down, share))
    pieces += [up, down]
    up, down = shift(up[:half], "z", 1), shift(down[half:], "z", -1)
    acc, dsq, nsq = inner(pos, noise_full, pieces)
    nsq = (jnp.sum(nsq, axis=1) / 4096)[None, :]
    dist = distance(pos, noise_full, up, down, acc, dsq, nsq)
    pieces += [up, down]

    noise_cols = lax.all_gather(share, plane, axis=0)
    dist_all = lax.all_gather(dist, "z", axis=0)
    dist_t = dist.T

    data_pot = jnp.zeros((rows,), F32)
    noise_pot = jnp.zeros((cols,), F32)
    for sweep in range(ITERS):
        scores = (data_pot[:, None] - dist) / EPSILON
        if sweep == 0:
            top = jnp.max(scores, axis=0)
            total = jnp.sum(jnp.exp(scores - top[None, :]), axis=0)
            top, total = row_total(jnp.stack([top, total]), merge)
        else:
            top = log_noise - noise_pot / EPSILON
            total = row_total(jnp.sum(jnp.exp(scores - top[None, :]), axis=0), add)
        noise_pot = EPSILON * log_noise - EPSILON * (top + jnp.log(total))
        scores = (noise_pot[None, :] - dist) / EPSILON
        if sweep == 0:
            top = jnp.max(scores, axis=1)
            total = jnp.sum(jnp.exp(scores - top[:, None]), axis=1)
            top, total = col_total(jnp.stack([top, total]), merge)
        else:
            top = log_data - data_pot / EPSILON
            total = jnp.sum(jnp.exp(scores - top[:, None]), axis=1)
            if sweep < ITERS - 1:
                total = col_total(total, add)
            else:
                both = [jnp.concatenate([total, noise_pot])]
                both += [swap(both[0], "z", k) for k in (1, 2, 3)]
                total = add([b[:rows] for b in both])
                both = jnp.concatenate([total] + [b[rows:] for b in both])
                far = swap(both, "z", 4)
                total = both[:rows] + far[:rows]
                pot_all = jnp.concatenate([both[rows:], far[rows:]])
        data_pot = EPSILON * log_data - EPSILON * (top + jnp.log(total))

    top = log_noise - noise_pot / EPSILON
    weight = jnp.exp((data_pot[None, :] - dist_t) / EPSILON - top[:, None])
    own_up, own_low, oth_up, oth_low = noise_part(pos, weight, pieces)
    up = (own_up + swap(oth_up, "c", 1)).reshape(4, 4, cols // 2, 128)
    low = (own_low + swap(oth_low, "c", 1)).reshape(4, 4, cols // 2, 128)
    row_sum = row_total(jnp.sum(weight, axis=1), add)
    up, low = scatter_sum(up, "x"), scatter_sum(low, "y")

    norm = (log_data - data_pot / EPSILON)[:, None]
    data_target = data_target_of(
        pos, dist_all, pot_all.reshape(8, 1, cols), norm, noise_cols
    )
    up, low, data_target = barrier((up, low, data_target))
    up, low = scatter_sum(up, "y"), scatter_sum(low, "x")
    noise_target = jnp.concatenate([up, low]) / row_sum[:, None]
    return (noise_target, data_target)


def solution(mesh):
    devices = mesh.devices.reshape(8, 4, 4, 2)
    torus = Mesh(devices, ("z", "y", "x", "c"))
    plane = ("y", "x", "c")
    return jax.shard_map(
        on_device,
        mesh=torus,
        in_specs=(P("z", plane), P(plane, "z")),
        out_specs=(P("z", plane), P(plane, "z")),
        check_vma=False,
    )
```

```python
import functools
import math

import jax
import jax.numpy as jnp
from jax import lax
from jax.experimental import pallas as pl
from jax.experimental.pallas import tpu as pltpu
from jax.sharding import Mesh, PartitionSpec as P

ITERS = 3
EPSILON = 0.02
VMEM_LIMIT = 56 * 1024 * 1024
BF16 = jnp.bfloat16
F32 = jnp.float32


def shift(v, axis, k):
    n = lax.axis_size(axis)
    return lax.ppermute(v, axis, [(i, (i + k) % n) for i in range(n)])


def swap(v, axis, k):
    n = lax.axis_size(axis)
    return lax.ppermute(v, axis, [(i, i ^ k) for i in range(n)])


def split(v):
    hi = v.astype(BF16)
    return hi, (v - hi.astype(F32)).astype(BF16)


def anywhere():
    return pl.BlockSpec(memory_space=pl.ANY)


def in_vmem():
    return pl.BlockSpec(memory_space=pltpu.VMEM)


def in_smem():
    return pl.BlockSpec(memory_space=pltpu.SMEM)


def params():
    return pltpu.CompilerParams(vmem_limit_bytes=VMEM_LIMIT)


def dot3(a, b, a_dim, b_dim):
    ah, al = split(a)
    bh, bl = split(b)
    return lax.dot_general(
        jnp.concatenate([ah, ah, al], axis=a_dim),
        jnp.concatenate([bh, bl, bh], axis=b_dim),
        (((a_dim,), (b_dim,)), ((), ())),
        preferred_element_type=F32,
    )


def lane_sums(v):
    return v[:, :128] + v[:, 128:256] + v[:, 256:384] + v[:, 384:]


def each(count, step):
    lax.fori_loop(0, count, lambda k, _: (step(k), 0)[1], 0)


OFFSETS = (0, 7, 1, 6, 2, 5, 3, 4)


def chunk_of(z, k):
    m = (k + 1) // 2
    return lax.rem(z + m + (k % 2) * (8 - 2 * m), 8)


def columns(z):
    return pl.ds(pl.multiple_of(z * 512, 512), 512)


def inner_kernel(pos, noise, *refs):
    pieces = refs[:7]
    acc, dsq, nsq, send, dacc, nacc, nbuf, dbuf, nsem, dsem, ssem = refs[7:]

    def fetch_noise(k):
        return pltpu.make_async_copy(
            noise.at[:, columns(chunk_of(pos[3], k))], nbuf.at[k], nsem.at[k]
        )

    def fetch_data(k, ref):
        return pltpu.make_async_copy(ref, dbuf.at[k], dsem.at[k])

    for k, ref in enumerate(pieces):
        fetch_noise(k).start()
        fetch_data(k, ref).start()
    fetch_noise(7).start()
    acc[...] = jnp.zeros_like(acc)
    dacc[...] = jnp.zeros_like(dacc)
    nacc[...] = jnp.zeros_like(nacc)

    def hand_on(k, j):
        lanes = pl.ds(pl.multiple_of(j * 256 + (1 - pos[0]) * 128, 128), 128)
        return pltpu.make_async_copy(
            dbuf.at[k, :, lanes], send.at[k, :, pl.ds(j * 128, 128)], ssem.at[k, j]
        )

    def step(k):
        fetch_noise(k).wait()
        fetch_data(k, pieces[0]).wait()
        for j in range(2):
            hand_on(k, j).start()
        n, d = nbuf[k], dbuf[k]
        acc[...] += dot3(n, d, 1, 1)
        dacc[...] += lane_sums(d * d)
        nacc[...] += lane_sums(n * n)

    each(7, step)
    fetch_noise(7).wait()
    n = nbuf[7]
    nsq[...] = jnp.sum(nacc[...] + lane_sums(n * n), axis=1, keepdims=True)
    dsq[...] = jnp.sum(dacc[...].T, axis=0, keepdims=True)

    def finish(k):
        for j in range(2):
            hand_on(k, j).wait()

    each(7, finish)


def inner(pos, noise, pieces):
    cols, rows = noise.shape[0], pieces[0].shape[0]
    return pl.pallas_call(
        inner_kernel,
        in_specs=[in_smem()] + [anywhere()] * 8,
        out_specs=[in_vmem()] * 3 + [anywhere()],
        out_shape=[
            jax.ShapeDtypeStruct((cols, rows), F32),
            jax.ShapeDtypeStruct((1, rows), F32),
            jax.ShapeDtypeStruct((cols, 1), F32),
            jax.ShapeDtypeStruct((7, rows, 256), F32),
        ],
        scratch_shapes=[
            pltpu.VMEM((rows, 128), F32),
            pltpu.VMEM((cols, 128), F32),
            pltpu.VMEM((8, cols, 512), F32),
            pltpu.VMEM((7, rows, 512), F32),
            pltpu.SemaphoreType.DMA((8,)),
            pltpu.SemaphoreType.DMA((7,)),
            pltpu.SemaphoreType.DMA((7, 2)),
        ],
        compiler_params=params(),
        cost_estimate=pl.CostEstimate(
            flops=6 * cols * rows * 3584, bytes_accessed=15 * 2**20, transcendentals=0
        ),
        name="inner_products",
    )(pos, noise, *pieces)


def distance_kernel(
    pos, noise, top, low, acc, dsq, nsq, dist, dist_t, send, nbuf, dbuf, sems, ssem
):
    half = top.shape[0]
    copies = [
        pltpu.make_async_copy(top, dbuf.at[:half], sems.at[0]),
        pltpu.make_async_copy(low, dbuf.at[half:], sems.at[1]),
        pltpu.make_async_copy(
            noise.at[:, columns(lax.rem(pos[3] + 4, 8))], nbuf, sems.at[2]
        ),
    ]
    for copy in copies:
        copy.start()
    for copy in copies:
        copy.wait()
    sends = []
    for j in range(2):
        lanes = pl.ds(pl.multiple_of(j * 256 + (1 - pos[0]) * 128, 128), 128)
        sends.append(
            pltpu.make_async_copy(
                dbuf.at[:, lanes], send.at[:, pl.ds(j * 128, 128)], ssem.at[j]
            )
        )
    for copy in sends:
        copy.start()
    d = dbuf[...]
    inner_prod = acc[...] + dot3(nbuf[...], d, 1, 1)
    data_sq = dsq[...] + jnp.sum(lane_sums(d * d).T, axis=0, keepdims=True)
    res = (nsq[...] + data_sq - 2.0 * inner_prod) * (1.0 / 4096)
    dist[...] = res
    dist_t[...] = res.T
    for copy in sends:
        copy.wait()


def distance(pos, noise, top, low, acc, dsq, nsq):
    cols, rows = acc.shape
    return pl.pallas_call(
        distance_kernel,
        in_specs=[in_smem()] + [anywhere()] * 3 + [in_vmem()] * 3,
        out_specs=[in_vmem(), in_vmem(), anywhere()],
        out_shape=[
            jax.ShapeDtypeStruct((cols, rows), F32),
            jax.ShapeDtypeStruct((rows, cols), F32),
            jax.ShapeDtypeStruct((rows, 256), F32),
        ],
        scratch_shapes=[
            pltpu.VMEM((cols, 512), F32),
            pltpu.VMEM((rows, 512), F32),
            pltpu.SemaphoreType.DMA((3,)),
            pltpu.SemaphoreType.DMA((2,)),
        ],
        compiler_params=params(),
        cost_estimate=pl.CostEstimate(
            flops=6 * cols * rows * 512, bytes_accessed=4 * 2**20, transcendentals=0
        ),
        name="distance",
    )(pos, noise, top, low, acc, dsq, nsq)


def noise_part_kernel(pos, w, sums, *refs):
    pieces, oth, oth_last = refs[:9], refs[9], refs[10]
    up, low, wcat, dbuf, obuf, dsem, osem, ssem = refs[11:]
    core, x, y, z = pos[0], pos[1], pos[2], pos[3]
    rows, depth = w.shape
    half, mine = rows // 2, depth // 2
    part = mine // 2

    def fetch(k, ref, first, sem):
        copies = []
        for j in range(2):
            lanes = pl.ds(pl.multiple_of(j * 256 + core * 128, 128), 128)
            at = dbuf.at[k, pl.ds(first, ref.shape[0]), pl.ds(j * 128, 128)]
            copies.append(pltpu.make_async_copy(ref.at[:, lanes], at, dsem.at[k, sem + j]))
        return copies

    def fetch_other(k, ref):
        return pltpu.make_async_copy(ref, dbuf.at[k, pl.ds(mine, mine)], dsem.at[k, 4])

    last = fetch(7, pieces[7], 0, 0) + fetch(7, pieces[8], part, 2)
    last.append(fetch_other(7, oth_last))
    for k in range(7):
        for copy in fetch(k, pieces[k], 0, 0):
            copy.start()
        fetch_other(k, oth.at[k]).start()
    for copy in last:
        copy.start()
    h, l = split(w[...])
    wcat[:, :depth] = h
    wcat[:, depth : 2 * depth] = h
    wcat[:, 2 * depth :] = l

    def stores(g):
        dy = lax.rem(g // 4 - y + 4, 4)
        dx = lax.rem(lax.rem(g, 4) - x + 4, 4)
        copies = []
        for k, (ref, slot) in enumerate(((up, dx * 4 + dy), (low, dy * 4 + dx))):
            copies.append(
                pltpu.make_async_copy(
                    obuf.at[g, pl.ds(k * half, half)],
                    ref.at[slot, pl.ds(0, half)],
                    osem.at[k, g],
                )
            )
            copies.append(
                pltpu.make_async_copy(
                    sums.at[k], ref.at[slot, pl.ds(half, 8)], ssem.at[k, g]
                )
            )
        return copies

    def step(k):
        h, l = split(dbuf[k])
        res = lax.dot_general(
            wcat[...],
            jnp.concatenate([h, l, h], axis=0),
            (((1,), (0,)), ((), ())),
            preferred_element_type=F32,
        )
        for j in range(2):
            g = 2 * chunk_of(z, k) + j
            obuf[g] = res[:, j * 128 : (j + 1) * 128]
            for copy in stores(g):
                copy.start()

    def fetched(k):
        for copy in fetch(k, pieces[0], 0, 0):
            copy.wait()
        fetch_other(k, oth_last).wait()
        step(k)

    each(7, fetched)
    for copy in last:
        copy.wait()
    step(7)

    def finish(g):
        for copy in stores(g):
            copy.wait()

    each(16, finish)


def noise_part(pos, w, sums, pieces, oth, oth_last):
    rows, depth = w.shape
    return pl.pallas_call(
        noise_part_kernel,
        in_specs=[in_smem(), in_vmem(), in_vmem()] + [anywhere()] * 11,
        out_specs=[anywhere()] * 2,
        out_shape=[jax.ShapeDtypeStruct((16, rows // 2 + 8, 128), F32)] * 2,
        scratch_shapes=[
            pltpu.VMEM((rows, 3 * depth), BF16),
            pltpu.VMEM((8, depth, 256), F32),
            pltpu.VMEM((16, rows, 128), F32),
            pltpu.SemaphoreType.DMA((8, 5)),
            pltpu.SemaphoreType.DMA((2, 16)),
            pltpu.SemaphoreType.DMA((2, 16)),
        ],
        compiler_params=params(),
        cost_estimate=pl.CostEstimate(
            flops=6 * rows * depth * 2048, bytes_accessed=12 * 2**20, transcendentals=0
        ),
        name="noise_part",
    )(pos, w, sums, *pieces, oth, oth_last)


def data_target_kernel(pos, dist, pot, norm, noise, out, dbuf, nbuf, dsem, nsem):
    def fetch(k):
        return (
            pltpu.make_async_copy(dist.at[k], dbuf.at[k], dsem.at[k]),
            pltpu.make_async_copy(noise.at[:, k], nbuf.at[k], nsem.at[k]),
        )

    def start(k):
        for copy in fetch(k):
            copy.start()

    each(8, start)
    out[...] = jnp.zeros_like(out)

    def step(k):
        for copy in fetch(k):
            copy.wait()
        own = pot[jnp.bitwise_xor(k, pos[3])]
        w = jnp.exp((own - dbuf[k]) / EPSILON - norm[...])
        n = nbuf[k]
        out[...] += dot3(w, n.reshape(n.shape[0] * n.shape[1], n.shape[2]), 1, 0)

    each(8, step)


def data_target_of(pos, dist, pot, norm, noise):
    _, rows, depth = dist.shape
    shares, _, share, width = noise.shape
    return pl.pallas_call(
        data_target_kernel,
        in_specs=[in_smem(), anywhere(), in_vmem(), in_vmem(), anywhere()],
        out_specs=in_vmem(),
        out_shape=jax.ShapeDtypeStruct((rows, width), F32),
        scratch_shapes=[
            pltpu.VMEM((8, rows, depth), F32),
            pltpu.VMEM((8, shares, share, width), F32),
            pltpu.SemaphoreType.DMA((8,)),
            pltpu.SemaphoreType.DMA((8,)),
        ],
        compiler_params=params(),
        cost_estimate=pl.CostEstimate(
            flops=6 * rows * depth * 8 * width,
            bytes_accessed=15 * 2**20,
            transcendentals=8 * rows * depth,
        ),
        name="data_target",
    )(pos, dist, pot, norm, noise)


def others(v, axis):
    return [shift(v, axis, k) for k in (1, 2, 3)]


def merge(parts):
    top = functools.reduce(jnp.maximum, [p[0] for p in parts])
    total = sum(p[1] * jnp.exp(p[0] - top) for p in parts)
    return jnp.stack([top, total])


def add(parts):
    return sum(parts)


def row_total(v, join):
    v = join([v] + others(v, "x"))
    return join([v] + others(v, "y"))


def col_total(v, join):
    v = join([v] + [swap(v, "z", k) for k in (1, 2, 3)])
    return join([v, swap(v, "z", 4)])


def scatter_far(chunks, axis):
    n = chunks[2].shape[0] // 2
    up = shift(chunks[2][:n], axis, 1)
    down = shift(chunks[2][n:], axis, -1)
    up = jnp.concatenate([chunks[1][:n] + up, chunks[1][n:]])
    down = jnp.concatenate([chunks[3][:n], chunks[3][n:] + down])
    return up, down


def on_device(noise, data):
    cols, rows = noise.shape[0], data.shape[0]
    log_noise = -math.log(cols * lax.axis_size("z"))
    log_data = -math.log(rows * 32)
    pos = jnp.stack([lax.axis_index(a).astype(jnp.int32) for a in ("c", "x", "y", "z")])
    barrier = lax.optimization_barrier
    plane = ("y", "x", "c")

    noise_full = lax.all_gather(noise, plane, axis=1, tiled=True)
    half = rows // 2
    up, down = shift(data, "z", 1), shift(data, "z", -1)
    share = noise.reshape(4, 4, 2, cols // 32, 128)
    share = lax.all_to_all(share, "c", 2, 3)
    share = lax.all_to_all(share, "x", 1, 2)
    up, down, share = barrier((up, down, share))
    pieces = [data, up, down]
    up, down = shift(up, "z", 1), shift(down, "z", -1)
    share = lax.all_to_all(share, "y", 0, 1).reshape(cols // 32, 8, 512)
    up, down, share = barrier((up, down, share))
    pieces += [up, down]
    up, down = shift(up, "z", 1), shift(down, "z", -1)
    share = lax.all_to_all(share, "z", 1, 0)
    up, down, share = barrier((up, down, share))
    pieces += [up, down]
    up, down = shift(up[:half], "z", 1), shift(down[half:], "z", -1)
    acc, dsq, nsq, send = inner(pos, noise_full, pieces)
    up, down, acc, send = barrier((up, down, acc, send))
    oth = swap(send, "c", 1)
    dist, dist_t, send = distance(pos, noise_full, up, down, acc, dsq, nsq)
    oth_last = swap(send, "c", 1)
    pieces += [up, down]

    noise_cols = lax.all_gather(share, plane, axis=0)
    dist_all = lax.all_gather(dist_t, "z", axis=0)
    oth, oth_last, other = barrier((oth, oth_last, swap(dist, "c", 1)))
    dist = jnp.concatenate([dist, other], axis=1)

    both_rows = 2 * rows
    data_pot = jnp.zeros((both_rows,), F32)
    noise_pot = jnp.zeros((cols,), F32)
    for sweep in range(ITERS):
        scores = (data_pot[None, :] - dist) / EPSILON
        if sweep == 0:
            top = jnp.max(scores, axis=1)
            total = jnp.sum(jnp.exp(scores - top[:, None]), axis=1)
            top, total = row_total(jnp.stack([top, total]), merge)
        else:
            top = log_noise - noise_pot / EPSILON
            total = row_total(jnp.sum(jnp.exp(scores - top[:, None]), axis=1), add)
        noise_pot = EPSILON * log_noise - EPSILON * (top + jnp.log(total))
        scores = (noise_pot[:, None] - dist) / EPSILON
        if sweep == 0:
            top = jnp.max(scores, axis=0)
            total = jnp.sum(jnp.exp(scores - top[None, :]), axis=0)
            top, total = col_total(jnp.stack([top, total]), merge)
        else:
            top = log_data - data_pot / EPSILON
            total = jnp.sum(jnp.exp(scores - top[None, :]), axis=0)
            if sweep < ITERS - 1:
                total = col_total(total, add)
            else:
                both = [jnp.concatenate([total, noise_pot])]
                both += [swap(both[0], "z", k) for k in (1, 2, 3)]
                total = add([b[:both_rows] for b in both])
                both = jnp.concatenate([total] + [b[both_rows:] for b in both])
                far = swap(both, "z", 4)
                total = both[:both_rows] + far[:both_rows]
                pot_all = jnp.concatenate([both[both_rows:], far[both_rows:]])
        data_pot = EPSILON * log_data - EPSILON * (top + jnp.log(total))

    top = log_noise - noise_pot / EPSILON
    weight = jnp.exp((data_pot[None, :] - dist) / EPSILON - top[:, None])
    half = cols // 2
    sums = jnp.sum(weight, axis=1).reshape(2, half // 128, 128)
    sums = jnp.pad(sums, ((0, 0), (0, 8 - half // 128), (0, 0)))
    up, low = noise_part(pos, weight, sums, pieces, oth, oth_last)
    up, low = up.reshape(4, 4, half + 8, 128), low.reshape(4, 4, half + 8, 128)
    up_far, low_far = scatter_far(up, "x"), scatter_far(low, "y")
    norm = (log_data - data_pot[:rows] / EPSILON)[:, None]
    data_target = data_target_of(
        pos, dist_all, pot_all.reshape(8, 1, cols), norm, noise_cols
    )
    near = [shift(up_far[0], "x", 1), shift(up_far[1], "x", -1)]
    near += [shift(low_far[0], "y", 1), shift(low_far[1], "y", -1)]
    near, data_target = barrier((near, data_target))
    up, low = up[0] + near[0] + near[1], low[0] + near[2] + near[3]
    up = up[0] + sum(shift(up[k], "y", k) for k in (1, 2, 3))
    low = low[0] + sum(shift(low[k], "x", k) for k in (1, 2, 3))
    noise_target = jnp.concatenate(
        [v[:half] / v[half : half + half // 128].reshape(half, 1) for v in (up, low)]
    )
    return (noise_target, data_target)


def solution(mesh):
    devices = mesh.devices.reshape(8, 4, 4, 2)
    torus = Mesh(devices, ("z", "y", "x", "c"))
    plane = ("y", "x", "c")
    return jax.shard_map(
        on_device,
        mesh=torus,
        in_specs=(P("z", plane), P(plane, "z")),
        out_specs=(P("z", plane), P(plane, "z")),
        check_vma=False,
    )
```

```python
import functools
import math

import jax
import jax.numpy as jnp
from jax import lax
from jax.experimental import pallas as pl
from jax.experimental.pallas import tpu as pltpu
from jax.sharding import Mesh, PartitionSpec as P

ITERS = 3
EPSILON = 0.02
BF16 = jnp.bfloat16
F32 = jnp.float32


def shift(v, axis, k):
    n = lax.axis_size(axis)
    return lax.ppermute(v, axis, [(i, (i + k) % n) for i in range(n)])


def swap(v, axis, k):
    n = lax.axis_size(axis)
    return lax.ppermute(v, axis, [(i, i ^ k) for i in range(n)])


def split(v):
    hi = v.astype(BF16)
    return hi, (v - hi.astype(F32)).astype(BF16)


def anywhere():
    return pl.BlockSpec(memory_space=pl.ANY)


def in_vmem():
    return pl.BlockSpec(memory_space=pltpu.VMEM)


def in_smem():
    return pl.BlockSpec(memory_space=pltpu.SMEM)


def params(mib):
    return pltpu.CompilerParams(vmem_limit_bytes=mib * 2**20)


def dot3(a, b, a_dim, b_dim):
    ah, al = split(a)
    bh, bl = split(b)
    return lax.dot_general(
        jnp.concatenate([ah, ah, al], axis=a_dim),
        jnp.concatenate([bh, bl, bh], axis=b_dim),
        (((a_dim,), (b_dim,)), ((), ())),
        preferred_element_type=F32,
    )


def lane_sums(v):
    return v[:, :128] + v[:, 128:256] + v[:, 256:384] + v[:, 384:]


def each(count, step):
    lax.fori_loop(0, count, lambda k, _: (step(k), 0)[1], 0)


OFFSETS = (0, 7, 1, 6, 2, 5, 3, 4)


def chunk_of(z, k):
    m = (k + 1) // 2
    return lax.rem(z + m + (k % 2) * (8 - 2 * m), 8)


def columns(z):
    return pl.ds(pl.multiple_of(z * 512, 512), 512)


def inner_kernel(pos, noise, *refs):
    pieces = refs[:7]
    acc, dsq, nsq, tail, send, dacc, nacc, nbuf, dbuf, nsem, dsem, ssem = refs[7:]

    def fetch_noise(k):
        return pltpu.make_async_copy(
            noise.at[:, columns(chunk_of(pos[3], k))], nbuf.at[k], nsem.at[k]
        )

    def fetch_data(k, ref):
        return pltpu.make_async_copy(ref, dbuf.at[k], dsem.at[k])

    for k, ref in enumerate(pieces):
        fetch_noise(k).start()
        fetch_data(k, ref).start()
    fetch_noise(7).start()
    acc[...] = jnp.zeros_like(acc)
    dacc[...] = jnp.zeros_like(dacc)
    nacc[...] = jnp.zeros_like(nacc)

    def hand_on(k, j):
        lanes = pl.ds(pl.multiple_of(j * 256 + (1 - pos[0]) * 128, 128), 128)
        return pltpu.make_async_copy(
            dbuf.at[k, :, lanes], send.at[k, :, pl.ds(j * 128, 128)], ssem.at[k, j]
        )

    def step(k):
        fetch_noise(k).wait()
        fetch_data(k, pieces[0]).wait()
        for j in range(2):
            hand_on(k, j).start()
        n, d = nbuf[k], dbuf[k]
        acc[...] += dot3(n, d, 1, 1)
        dacc[...] += lane_sums(d * d)
        nacc[...] += lane_sums(n * n)

    each(7, step)
    fetch_noise(7).wait()
    n = nbuf[7]
    h, l = split(n)
    tail[...] = jnp.concatenate([h, l, h], axis=1)
    nsq[...] = jnp.sum(nacc[...] + lane_sums(n * n), axis=1, keepdims=True)
    dsq[...] = jnp.sum(dacc[...].T, axis=0, keepdims=True)

    def finish(k):
        for j in range(2):
            hand_on(k, j).wait()

    each(7, finish)


def inner(pos, noise, pieces):
    cols, rows = noise.shape[0], pieces[0].shape[0]
    return pl.pallas_call(
        inner_kernel,
        in_specs=[in_smem()] + [anywhere()] * 8,
        out_specs=[in_vmem()] * 4 + [anywhere()],
        out_shape=[
            jax.ShapeDtypeStruct((cols, rows), F32),
            jax.ShapeDtypeStruct((1, rows), F32),
            jax.ShapeDtypeStruct((cols, 1), F32),
            jax.ShapeDtypeStruct((cols, 1536), BF16),
            jax.ShapeDtypeStruct((7, rows, 256), F32),
        ],
        scratch_shapes=[
            pltpu.VMEM((rows, 128), F32),
            pltpu.VMEM((cols, 128), F32),
            pltpu.VMEM((8, cols, 512), F32),
            pltpu.VMEM((7, rows, 512), F32),
            pltpu.SemaphoreType.DMA((8,)),
            pltpu.SemaphoreType.DMA((7,)),
            pltpu.SemaphoreType.DMA((7, 2)),
        ],
        compiler_params=params(56),
        cost_estimate=pl.CostEstimate(
            flops=6 * cols * rows * 3584, bytes_accessed=15 * 2**20, transcendentals=0
        ),
        name="inner_products",
    )(pos, noise, *pieces)


def distance_kernel(pos, dsq, *refs):
    sources, outs, held, sems = refs[:5], refs[5:8], refs[8:13], refs[13]
    dist, dist_t, send = outs
    copies = [
        pltpu.make_async_copy(source, at, sems.at[k])
        for k, (source, at) in enumerate(zip(sources, held))
    ]
    for copy in copies:
        copy.start()
    for copy in copies:
        copy.wait()
    tail, top, low, acc, nsq = held
    d = jnp.concatenate([top[...], low[...]], axis=0)
    h, l = split(d)
    inner_prod = acc[...] + lax.dot_general(
        tail[...],
        jnp.concatenate([h, h, l], axis=1),
        (((1,), (1,)), ((), ())),
        preferred_element_type=F32,
    )
    data_sq = dsq[...] + jnp.sum(lane_sums(d * d).T, axis=0, keepdims=True)
    res = (nsq[...] + data_sq - 2.0 * inner_prod) * (1.0 / 4096)
    dist[...] = res
    dist_t[...] = res.T
    for j in range(2):
        first = d[:, j * 256 : j * 256 + 128]
        second = d[:, j * 256 + 128 : j * 256 + 256]
        send[:, j * 128 : (j + 1) * 128] = jnp.where(pos[0] == 0, second, first)


def distance(pos, tail, top, low, acc, dsq, nsq):
    cols, rows = acc.shape
    return pl.pallas_call(
        distance_kernel,
        in_specs=[in_smem(), in_vmem()] + [anywhere()] * 5,
        out_specs=[in_vmem()] * 3,
        out_shape=[
            jax.ShapeDtypeStruct((cols, rows), F32),
            jax.ShapeDtypeStruct((rows, cols), F32),
            jax.ShapeDtypeStruct((rows, 256), F32),
        ],
        scratch_shapes=[
            pltpu.VMEM((cols, 1536), BF16),
            pltpu.VMEM((rows // 2, 512), F32),
            pltpu.VMEM((rows // 2, 512), F32),
            pltpu.VMEM((cols, rows), F32),
            pltpu.VMEM((cols, 1), F32),
            pltpu.SemaphoreType.DMA((5,)),
        ],
        compiler_params=params(56),
        cost_estimate=pl.CostEstimate(
            flops=6 * cols * rows * 512, bytes_accessed=4 * 2**20, transcendentals=0
        ),
        name="distance",
    )(pos, dsq, tail, top, low, acc, nsq)


def noise_part_kernel(pos, dist, pot, norm, *refs):
    pieces, oth, oth_last = refs[:9], refs[9], refs[10]
    up, low, wcat, dbuf, obuf, sums, dsem, osem, ssem = refs[11:]
    core, x, y, z = pos[0], pos[1], pos[2], pos[3]
    rows, depth = dist.shape
    half, mine = rows // 2, depth // 2
    part = mine // 2

    def fetch(k, ref, first, sem):
        copies = []
        for j in range(2):
            lanes = pl.ds(pl.multiple_of(j * 256 + core * 128, 128), 128)
            at = dbuf.at[k, pl.ds(first, ref.shape[0]), pl.ds(j * 128, 128)]
            copies.append(pltpu.make_async_copy(ref.at[:, lanes], at, dsem.at[k, sem + j]))
        return copies

    def fetch_other(k, ref):
        return pltpu.make_async_copy(ref, dbuf.at[k, pl.ds(mine, mine)], dsem.at[k, 4])

    last = fetch(7, pieces[7], 0, 0) + fetch(7, pieces[8], part, 2)
    last.append(fetch_other(7, oth_last))
    for k in range(7):
        for copy in fetch(k, pieces[k], 0, 0):
            copy.start()
        fetch_other(k, oth.at[k]).start()
    for copy in last:
        copy.start()
    h, l = split(jnp.exp((pot[...] - dist[...]) / EPSILON - norm[...]))
    wcat[:, :depth] = h
    wcat[:, depth : 2 * depth] = h
    wcat[:, 2 * depth :] = l
    total = lax.dot_general(
        jnp.ones((8, 2 * depth), BF16),
        wcat[:, depth:],
        (((1,), (1,)), ((), ())),
        preferred_element_type=F32,
    )
    for k in range(2):
        for j in range(half // 128):
            first = k * half + j * 128
            sums[k, j : j + 1, :] = total[:1, first : first + 128]
        sums[k, half // 128 :, :] = jnp.zeros((8 - half // 128, 128), F32)

    def stores(g):
        dy = lax.rem(g // 4 - y + 4, 4)
        dx = lax.rem(lax.rem(g, 4) - x + 4, 4)
        copies = []
        for k, (ref, slot) in enumerate(((up, dx * 4 + dy), (low, dy * 4 + dx))):
            copies.append(
                pltpu.make_async_copy(
                    obuf.at[g, pl.ds(k * half, half)],
                    ref.at[slot, pl.ds(0, half)],
                    osem.at[k, g],
                )
            )
            copies.append(
                pltpu.make_async_copy(
                    sums.at[k], ref.at[slot, pl.ds(half, 8)], ssem.at[k, g]
                )
            )
        return copies

    def step(k):
        h, l = split(dbuf[k])
        res = lax.dot_general(
            wcat[...],
            jnp.concatenate([h, l, h], axis=0),
            (((1,), (0,)), ((), ())),
            preferred_element_type=F32,
        )
        for j in range(2):
            g = 2 * chunk_of(z, k) + j
            obuf[g] = res[:, j * 128 : (j + 1) * 128]
            for copy in stores(g):
                copy.start()

    def fetched(k):
        for copy in fetch(k, pieces[0], 0, 0):
            copy.wait()
        fetch_other(k, oth_last).wait()
        step(k)

    each(7, fetched)
    for copy in last:
        copy.wait()
    step(7)

    def finish(g):
        for copy in stores(g):
            copy.wait()

    each(16, finish)


def noise_part(pos, dist, pot, norm, pieces, oth, oth_last):
    rows, depth = dist.shape
    return pl.pallas_call(
        noise_part_kernel,
        in_specs=[in_smem()] + [in_vmem()] * 3 + [anywhere()] * 11,
        out_specs=[anywhere()] * 2,
        out_shape=[jax.ShapeDtypeStruct((16, rows // 2 + 8, 128), F32)] * 2,
        scratch_shapes=[
            pltpu.VMEM((rows, 3 * depth), BF16),
            pltpu.VMEM((8, depth, 256), F32),
            pltpu.VMEM((16, rows, 128), F32),
            pltpu.VMEM((2, 8, 128), F32),
            pltpu.SemaphoreType.DMA((8, 5)),
            pltpu.SemaphoreType.DMA((2, 16)),
            pltpu.SemaphoreType.DMA((2, 16)),
        ],
        compiler_params=params(56),
        cost_estimate=pl.CostEstimate(
            flops=6 * rows * depth * 2048, bytes_accessed=12 * 2**20, transcendentals=0
        ),
        name="noise_part",
    )(pos, dist, pot, norm, *pieces, oth, oth_last)


def slot_of(k):
    return jnp.where(k < 4, k, 11 - k)


def data_target_kernel(pos, dist, pot, norm, noise, out, dbuf, nbuf, dsem, nsem):
    def fetch(k):
        return (
            pltpu.make_async_copy(dist.at[k], dbuf.at[k], dsem.at[k]),
            pltpu.make_async_copy(noise.at[:, k], nbuf.at[k], nsem.at[k]),
        )

    def start(k):
        for copy in fetch(k):
            copy.start()

    each(8, start)
    out[...] = jnp.zeros_like(out)

    def step(k):
        for copy in fetch(k):
            copy.wait()
        own = pot[slot_of(jnp.bitwise_xor(k, pos[3]))]
        w = jnp.exp((own - dbuf[k]) / EPSILON - norm[...])
        n = nbuf[k]
        out[...] += dot3(w, n.reshape(n.shape[0] * n.shape[1], n.shape[2]), 1, 0)

    each(8, step)


def data_target_of(pos, dist, pot, norm, noise):
    _, rows, depth = dist.shape
    shares, _, share, width = noise.shape
    return pl.pallas_call(
        data_target_kernel,
        in_specs=[in_smem(), anywhere(), in_vmem(), in_vmem(), anywhere()],
        out_specs=in_vmem(),
        out_shape=jax.ShapeDtypeStruct((rows, width), F32),
        scratch_shapes=[
            pltpu.VMEM((8, rows, depth), F32),
            pltpu.VMEM((8, shares, share, width), F32),
            pltpu.SemaphoreType.DMA((8,)),
            pltpu.SemaphoreType.DMA((8,)),
        ],
        compiler_params=params(56),
        cost_estimate=pl.CostEstimate(
            flops=6 * rows * depth * 8 * width,
            bytes_accessed=15 * 2**20,
            transcendentals=8 * rows * depth,
        ),
        name="data_target",
    )(pos, dist, pot, norm, noise)


def others(v, axis):
    return [swap(v, axis, k) for k in (1, 2, 3)]


def merge(parts):
    top = functools.reduce(jnp.maximum, [p[0] for p in parts])
    total = sum(p[1] * jnp.exp(p[0] - top) for p in parts)
    return jnp.stack([top, total])


def add(parts):
    return sum(parts)


def row_total(v, join):
    v = join([v] + others(v, "x"))
    return join([v] + others(v, "y"))


def col_total(v, join):
    v = join([v] + [swap(v, "z", k) for k in (1, 2, 3)])
    return join([v, swap(v, "z", 7)])


def scatter_far(chunks, axis):
    n = chunks[2].shape[0] // 2
    up = shift(chunks[2][:n], axis, 1)
    down = shift(chunks[2][n:], axis, -1)
    up = jnp.concatenate([chunks[1][:n] + up, chunks[1][n:]])
    down = jnp.concatenate([chunks[3][:n], chunks[3][n:] + down])
    return up, down


def on_device(noise, data):
    cols, rows = noise.shape[0], data.shape[0]
    log_noise = -math.log(cols * lax.axis_size("z"))
    log_data = -math.log(rows * 32)
    pos = jnp.stack([lax.axis_index(a).astype(jnp.int32) for a in ("c", "x", "y", "z")])
    barrier = lax.optimization_barrier
    plane = ("y", "x", "c")

    noise_full = lax.all_gather(noise, plane, axis=1, tiled=True)
    half = rows // 2
    up, down = shift(data, "z", 1), shift(data, "z", -1)
    share = noise.reshape(4, 4, 2, cols // 32, 128)
    share = lax.all_to_all(share, "c", 2, 3)
    share = lax.all_to_all(share, "x", 1, 2)
    up, down, share = barrier((up, down, share))
    pieces = [data, up, down]
    up, down = shift(up, "z", 1), shift(down, "z", -1)
    share = lax.all_to_all(share, "y", 0, 1).reshape(cols // 32, 8, 512)
    up, down, share = barrier((up, down, share))
    pieces += [up, down]
    up, down = shift(up, "z", 1), shift(down, "z", -1)
    share = lax.all_to_all(share, "z", 1, 0)
    up, down, share = barrier((up, down, share))
    pieces += [up, down]
    up, down = shift(up[:half], "z", 1), shift(down[half:], "z", -1)
    acc, dsq, nsq, tail, send = inner(pos, noise_full, pieces)
    up, down, acc, send = barrier((up, down, acc, send))
    oth = swap(send, "c", 1)
    dist, dist_t, send = distance(pos, tail, up, down, acc, dsq, nsq)
    oth_last = swap(send, "c", 1)
    pieces += [up, down]

    noise_cols = lax.all_gather(share, plane, axis=0)
    dist_all = lax.all_gather(dist_t, "z", axis=0)
    oth, oth_last, other = barrier((oth, oth_last, swap(dist, "c", 1)))
    dist = jnp.concatenate([dist, other], axis=1)

    both_rows = 2 * rows
    data_pot = jnp.zeros((both_rows,), F32)
    noise_pot = jnp.zeros((cols,), F32)
    for sweep in range(ITERS):
        scores = (data_pot[None, :] - dist) / EPSILON
        if sweep == 0:
            top = jnp.max(scores, axis=1)
            total = jnp.sum(jnp.exp(scores - top[:, None]), axis=1)
            top, total = row_total(jnp.stack([top, total]), merge)
        else:
            top = log_noise - noise_pot / EPSILON
            total = row_total(jnp.sum(jnp.exp(scores - top[:, None]), axis=1), add)
        noise_pot = EPSILON * log_noise - EPSILON * (top + jnp.log(total))
        scores = (noise_pot[:, None] - dist) / EPSILON
        if sweep == 0:
            top = jnp.max(scores, axis=0)
            total = jnp.sum(jnp.exp(scores - top[None, :]), axis=0)
            top, total = col_total(jnp.stack([top, total]), merge)
        else:
            top = log_data - data_pot / EPSILON
            total = jnp.sum(jnp.exp(scores - top[None, :]), axis=0)
            if sweep < ITERS - 1:
                total = col_total(total, add)
            else:
                both = [jnp.concatenate([total, noise_pot])]
                both += [swap(both[0], "z", k) for k in (1, 2, 3)]
                total = add([b[:both_rows] for b in both])
                both = jnp.concatenate([total] + [b[both_rows:] for b in both])
                far = swap(both, "z", 7)
                total = both[:both_rows] + far[:both_rows]
                pot_all = jnp.concatenate([both[both_rows:], far[both_rows:]])
        data_pot = EPSILON * log_data - EPSILON * (top + jnp.log(total))

    half = cols // 2
    norm = (log_noise - noise_pot / EPSILON)[:, None]
    up, low = noise_part(pos, dist, data_pot[None, :], norm, pieces, oth, oth_last)
    up, low = up.reshape(4, 4, half + 8, 128), low.reshape(4, 4, half + 8, 128)
    up_far, low_far = scatter_far(up, "x"), scatter_far(low, "y")
    norm = (log_data - data_pot[:rows] / EPSILON)[:, None]
    data_target = data_target_of(
        pos, dist_all, pot_all.reshape(8, 1, cols), norm, noise_cols
    )
    near = [shift(up_far[0], "x", 1), shift(up_far[1], "x", -1)]
    near += [shift(low_far[0], "y", 1), shift(low_far[1], "y", -1)]
    near, data_target = barrier((near, data_target))
    up, low = up[0] + near[0] + near[1], low[0] + near[2] + near[3]
    up = up[0] + sum(shift(up[k], "y", k) for k in (1, 2, 3))
    low = low[0] + sum(shift(low[k], "x", k) for k in (1, 2, 3))
    noise_target = jnp.concatenate(
        [v[:half] / v[half : half + half // 128].reshape(half, 1) for v in (up, low)]
    )
    return (noise_target, data_target)


def solution(mesh):
    devices = mesh.devices.reshape(8, 4, 4, 2)
    torus = Mesh(devices, ("z", "y", "x", "c"))
    plane = ("y", "x", "c")
    return jax.shard_map(
        on_device,
        mesh=torus,
        in_specs=(P("z", plane), P(plane, "z")),
        out_specs=(P("z", plane), P(plane, "z")),
        check_vma=False,
    )
```

```python
import functools
import math

import jax
import jax.numpy as jnp
from jax import lax
from jax.experimental import pallas as pl
from jax.experimental.pallas import tpu as pltpu
from jax.sharding import Mesh, PartitionSpec as P

ITERS = 3
EPSILON = 0.02
BF16 = jnp.bfloat16
F32 = jnp.float32


def shift(v, axis, k):
    n = lax.axis_size(axis)
    return lax.ppermute(v, axis, [(i, (i + k) % n) for i in range(n)])


def swap(v, axis, k):
    n = lax.axis_size(axis)
    return lax.ppermute(v, axis, [(i, i ^ k) for i in range(n)])


def split(v):
    hi = v.astype(BF16)
    return hi, (v - hi.astype(F32)).astype(BF16)


def anywhere():
    return pl.BlockSpec(memory_space=pl.ANY)


def in_vmem():
    return pl.BlockSpec(memory_space=pltpu.VMEM)


def in_smem():
    return pl.BlockSpec(memory_space=pltpu.SMEM)


def params(mib):
    return pltpu.CompilerParams(vmem_limit_bytes=mib * 2**20)


def dot3(a, b, a_dim, b_dim):
    ah, al = split(a)
    bh, bl = split(b)
    return lax.dot_general(
        jnp.concatenate([ah, ah, al], axis=a_dim),
        jnp.concatenate([bh, bl, bh], axis=b_dim),
        (((a_dim,), (b_dim,)), ((), ())),
        preferred_element_type=F32,
    )


def lane_sums(v):
    return v[:, :128] + v[:, 128:256] + v[:, 256:384] + v[:, 384:]


def each(count, step):
    lax.fori_loop(0, count, lambda k, _: (step(k), 0)[1], 0)


OFFSETS = (0, 7, 1, 6, 2, 5, 3, 4)


def chunk_of(z, k):
    m = (k + 1) // 2
    return lax.rem(z + m + (k % 2) * (8 - 2 * m), 8)


def columns(z):
    return pl.ds(pl.multiple_of(z * 512, 512), 512)


def inner_kernel(pos, noise, *refs):
    pieces = refs[:7]
    acc, dsq, nsq, send, dacc, nacc, nbuf, dbuf, nsem, dsem, ssem = refs[7:]

    def fetch_noise(k):
        return pltpu.make_async_copy(
            noise.at[:, columns(chunk_of(pos[3], k))], nbuf.at[k], nsem.at[k]
        )

    def fetch_data(k, ref):
        return pltpu.make_async_copy(ref, dbuf.at[k], dsem.at[k])

    for k, ref in enumerate(pieces):
        fetch_noise(k).start()
        fetch_data(k, ref).start()
    fetch_noise(7).start()
    acc[...] = jnp.zeros_like(acc)
    dacc[...] = jnp.zeros_like(dacc)
    nacc[...] = jnp.zeros_like(nacc)

    def hand_on(k, j):
        lanes = pl.ds(pl.multiple_of(j * 256 + (1 - pos[0]) * 128, 128), 128)
        return pltpu.make_async_copy(
            dbuf.at[k, :, lanes], send.at[k, :, pl.ds(j * 128, 128)], ssem.at[k, j]
        )

    def step(k):
        fetch_noise(k).wait()
        fetch_data(k, pieces[0]).wait()
        for j in range(2):
            hand_on(k, j).start()
        n, d = nbuf[k], dbuf[k]
        acc[...] += dot3(n, d, 1, 1)
        dacc[...] += lane_sums(d * d)
        nacc[...] += lane_sums(n * n)

    each(7, step)
    fetch_noise(7).wait()
    n = nbuf[7]
    nsq[...] = jnp.sum(nacc[...] + lane_sums(n * n), axis=1, keepdims=True)
    dsq[...] = jnp.sum(dacc[...].T, axis=0, keepdims=True)

    def finish(k):
        for j in range(2):
            hand_on(k, j).wait()

    each(7, finish)


def inner(pos, noise, pieces):
    cols, rows = noise.shape[0], pieces[0].shape[0]
    return pl.pallas_call(
        inner_kernel,
        in_specs=[in_smem()] + [anywhere()] * 8,
        out_specs=[in_vmem()] * 3 + [anywhere()],
        out_shape=[
            jax.ShapeDtypeStruct((cols, rows), F32),
            jax.ShapeDtypeStruct((1, rows), F32),
            jax.ShapeDtypeStruct((cols, 1), F32),
            jax.ShapeDtypeStruct((7, rows, 256), F32),
        ],
        scratch_shapes=[
            pltpu.VMEM((rows, 128), F32),
            pltpu.VMEM((cols, 128), F32),
            pltpu.VMEM((8, cols, 512), F32),
            pltpu.VMEM((7, rows, 512), F32),
            pltpu.SemaphoreType.DMA((8,)),
            pltpu.SemaphoreType.DMA((7,)),
            pltpu.SemaphoreType.DMA((7, 2)),
        ],
        compiler_params=params(56),
        cost_estimate=pl.CostEstimate(
            flops=6 * cols * rows * 3584, bytes_accessed=15 * 2**20, transcendentals=0
        ),
        name="inner_products",
    )(pos, noise, *pieces)


def distance_kernel(pos, dsq, *refs):
    sources, outs, held, sems = refs[:5], refs[5:8], refs[8:13], refs[13]
    sources = (sources[0].at[:, columns(lax.rem(pos[3] + 4, 8))],) + sources[1:]
    dist, dist_t, send = outs
    copies = [
        pltpu.make_async_copy(source, at, sems.at[k])
        for k, (source, at) in enumerate(zip(sources, held))
    ]
    for copy in copies:
        copy.start()
    for copy in copies:
        copy.wait()
    noise, top, low, acc, nsq = held
    d = jnp.concatenate([top[...], low[...]], axis=0)
    inner_prod = acc[...] + dot3(noise[...], d, 1, 1)
    data_sq = dsq[...] + jnp.sum(lane_sums(d * d).T, axis=0, keepdims=True)
    res = (nsq[...] + data_sq - 2.0 * inner_prod) * (1.0 / 4096)
    dist[...] = res
    dist_t[...] = res.T
    for j in range(2):
        first = d[:, j * 256 : j * 256 + 128]
        second = d[:, j * 256 + 128 : j * 256 + 256]
        send[:, j * 128 : (j + 1) * 128] = jnp.where(pos[0] == 0, second, first)


def distance(pos, noise, top, low, acc, dsq, nsq):
    cols, rows = acc.shape
    return pl.pallas_call(
        distance_kernel,
        in_specs=[in_smem(), in_vmem()] + [anywhere()] * 5,
        out_specs=[in_vmem()] * 3,
        out_shape=[
            jax.ShapeDtypeStruct((cols, rows), F32),
            jax.ShapeDtypeStruct((rows, cols), F32),
            jax.ShapeDtypeStruct((rows, 256), F32),
        ],
        scratch_shapes=[
            pltpu.VMEM((cols, 512), F32),
            pltpu.VMEM((rows // 2, 512), F32),
            pltpu.VMEM((rows // 2, 512), F32),
            pltpu.VMEM((cols, rows), F32),
            pltpu.VMEM((cols, 1), F32),
            pltpu.SemaphoreType.DMA((5,)),
        ],
        compiler_params=params(56),
        cost_estimate=pl.CostEstimate(
            flops=6 * cols * rows * 512, bytes_accessed=4 * 2**20, transcendentals=0
        ),
        name="distance",
    )(pos, dsq, noise, top, low, acc, nsq)


def noise_part_kernel(pos, dist, pot, norm, *refs):
    pieces, oth, oth_last = refs[:9], refs[9], refs[10]
    up, low, far, refs = refs[11], refs[12], refs[13:17], refs[17:]
    wcat, dbuf, obuf, sums, dsem, osem, ssem, fsem = refs
    core, x, y, z = pos[0], pos[1], pos[2], pos[3]
    rows, depth = dist.shape
    half, mine = rows // 2, depth // 2
    part = mine // 2

    def fetch(k, ref, first, sem):
        copies = []
        for j in range(2):
            lanes = pl.ds(pl.multiple_of(j * 256 + core * 128, 128), 128)
            at = dbuf.at[k, pl.ds(first, ref.shape[0]), pl.ds(j * 128, 128)]
            copies.append(pltpu.make_async_copy(ref.at[:, lanes], at, dsem.at[k, sem + j]))
        return copies

    def fetch_other(k, ref):
        return pltpu.make_async_copy(ref, dbuf.at[k, pl.ds(mine, mine)], dsem.at[k, 4])

    last = fetch(7, pieces[7], 0, 0) + fetch(7, pieces[8], part, 2)
    last.append(fetch_other(7, oth_last))
    for k in range(7):
        for copy in fetch(k, pieces[k], 0, 0):
            copy.start()
        fetch_other(k, oth.at[k]).start()
    for copy in last:
        copy.start()
    h, l = split(jnp.exp((pot[...] - dist[...]) / EPSILON - norm[...]))
    wcat[:, :depth] = h
    wcat[:, depth : 2 * depth] = h
    wcat[:, 2 * depth :] = l
    total = lax.dot_general(
        jnp.ones((8, 2 * depth), BF16),
        wcat[:, depth:],
        (((1,), (1,)), ((), ())),
        preferred_element_type=F32,
    )
    for k in range(2):
        for j in range(half // 128):
            first = k * half + j * 128
            sums[k, j : j + 1, :] = total[:1, first : first + 128]
        sums[k, half // 128 :, :] = jnp.zeros((8 - half // 128, 128), F32)

    def place(g, k, ref, slot, sem):
        return (
            pltpu.make_async_copy(
                obuf.at[g, pl.ds(k * half, half)], ref.at[slot, pl.ds(0, half)], sem[0]
            ),
            pltpu.make_async_copy(
                sums.at[k], ref.at[slot, pl.ds(half, 8)], sem[1]
            ),
        )

    def stores(g, act):
        dy = lax.rem(g // 4 - y + 4, 4)
        dx = lax.rem(lax.rem(g, 4) - x + 4, 4)
        for k, (ref, major, minor) in enumerate(((up, dx, dy), (low, dy, dx))):
            sem = (osem.at[k, g], ssem.at[k, g])
            for copy in place(g, k, ref, major * 4 + minor, sem):
                act(copy)
            for j in range(2):
                sem = (fsem.at[k, minor, 0], fsem.at[k, minor, 1])

                @pl.when((major == 2) & (minor // 2 == j))
                def _():
                    slot = lax.rem(minor, 2)
                    for copy in place(g, k, far[2 * k + j], slot, sem):
                        act(copy)

    def step(k):
        h, l = split(dbuf[k])
        res = lax.dot_general(
            wcat[...],
            jnp.concatenate([h, l, h], axis=0),
            (((1,), (0,)), ((), ())),
            preferred_element_type=F32,
        )
        for j in range(2):
            g = 2 * chunk_of(z, k) + j
            obuf[g] = res[:, j * 128 : (j + 1) * 128]
            stores(g, lambda copy: copy.start())

    def fetched(k):
        for copy in fetch(k, pieces[0], 0, 0):
            copy.wait()
        fetch_other(k, oth_last).wait()
        step(k)

    each(7, fetched)
    for copy in last:
        copy.wait()
    step(7)

    each(16, lambda g: stores(g, lambda copy: copy.wait()))


def noise_part(pos, dist, pot, norm, pieces, oth, oth_last):
    rows, depth = dist.shape
    return pl.pallas_call(
        noise_part_kernel,
        in_specs=[in_smem()] + [in_vmem()] * 3 + [anywhere()] * 11,
        out_specs=[anywhere()] * 6,
        out_shape=[jax.ShapeDtypeStruct((16, rows // 2 + 8, 128), F32)] * 2
        + [jax.ShapeDtypeStruct((2, rows // 2 + 8, 128), F32)] * 4,
        scratch_shapes=[
            pltpu.VMEM((rows, 3 * depth), BF16),
            pltpu.VMEM((8, depth, 256), F32),
            pltpu.VMEM((16, rows, 128), F32),
            pltpu.VMEM((2, 8, 128), F32),
            pltpu.SemaphoreType.DMA((8, 5)),
            pltpu.SemaphoreType.DMA((2, 16)),
            pltpu.SemaphoreType.DMA((2, 16)),
            pltpu.SemaphoreType.DMA((2, 4, 2)),
        ],
        compiler_params=params(56),
        cost_estimate=pl.CostEstimate(
            flops=6 * rows * depth * 2048, bytes_accessed=12 * 2**20, transcendentals=0
        ),
        name="noise_part",
    )(pos, dist, pot, norm, *pieces, oth, oth_last)


def slot_of(k):
    return jnp.where(k < 4, k, 11 - k)


def data_target_kernel(pos, dist, pot, norm, noise, out, dbuf, nbuf, dsem, nsem):
    def fetch(k):
        copies = [pltpu.make_async_copy(dist.at[k], dbuf.at[k], dsem.at[k])]
        for c in range(2):
            for j in range(2):
                lanes = pl.ds(j * 256 + c * 128, 128)
                copies.append(
                    pltpu.make_async_copy(
                        noise.at[:, c, k, :, pl.ds(j * 128, 128)],
                        nbuf.at[k, :, :, lanes],
                        nsem.at[k, 2 * c + j],
                    )
                )
        return copies

    def start(k):
        for copy in fetch(k):
            copy.start()

    each(8, start)
    out[...] = jnp.zeros_like(out)

    def step(k):
        for copy in fetch(k):
            copy.wait()
        own = pot[slot_of(jnp.bitwise_xor(k, pos[3]))]
        w = jnp.exp((own - dbuf[k]) / EPSILON - norm[...])
        n = nbuf[k]
        out[...] += dot3(w, n.reshape(n.shape[0] * n.shape[1], n.shape[2]), 1, 0)

    each(8, step)


def data_target_of(pos, dist, pot, norm, noise):
    _, rows, depth = dist.shape
    shares, _, _, share, _ = noise.shape
    width = 512
    return pl.pallas_call(
        data_target_kernel,
        in_specs=[in_smem(), anywhere(), in_vmem(), in_vmem(), anywhere()],
        out_specs=in_vmem(),
        out_shape=jax.ShapeDtypeStruct((rows, width), F32),
        scratch_shapes=[
            pltpu.VMEM((8, rows, depth), F32),
            pltpu.VMEM((8, shares, share, width), F32),
            pltpu.SemaphoreType.DMA((8,)),
            pltpu.SemaphoreType.DMA((8, 4)),
        ],
        compiler_params=params(56),
        cost_estimate=pl.CostEstimate(
            flops=6 * rows * depth * 8 * width,
            bytes_accessed=15 * 2**20,
            transcendentals=8 * rows * depth,
        ),
        name="data_target",
    )(pos, dist, pot, norm, noise)


def others(v, axis):
    return [swap(v, axis, k) for k in (1, 2, 3)]


def merge(parts):
    top = functools.reduce(jnp.maximum, [p[0] for p in parts])
    total = sum(p[1] * jnp.exp(p[0] - top) for p in parts)
    return jnp.stack([top, total])


def add(parts):
    return sum(parts)


def row_total(v, join):
    v = join([v] + others(v, "x"))
    return join([v] + others(v, "y"))


def col_total(v, join):
    v = join([v] + [swap(v, "z", k) for k in (1, 2, 3)])
    return join([v, swap(v, "z", 7)])


def scatter_far(chunks, far, axis):
    n = far[0].shape[0]
    up, down = shift(far[0], axis, 1), shift(far[1], axis, -1)
    up = jnp.concatenate([chunks[1][:n] + up, chunks[1][n:]])
    down = jnp.concatenate([chunks[3][:n], chunks[3][n:] + down])
    return up, down


def on_device(noise, data):
    cols, rows = noise.shape[0], data.shape[0]
    log_noise = -math.log(cols * lax.axis_size("z"))
    log_data = -math.log(rows * 32)
    pos = jnp.stack([lax.axis_index(a).astype(jnp.int32) for a in ("c", "x", "y", "z")])
    barrier = lax.optimization_barrier
    plane = ("y", "x", "c")

    noise_full = lax.all_gather(noise, plane, axis=1, tiled=True)
    half = rows // 2
    up, down = shift(data, "z", 1), shift(data, "z", -1)
    share = lax.all_to_all(noise.reshape(4, 4, cols // 16, 128), "x", 1, 2)
    up, down, share = barrier((up, down, share))
    pieces = [data, up, down]
    up, down = shift(up, "z", 1), shift(down, "z", -1)
    share = lax.all_to_all(share, "y", 0, 1).reshape(cols // 16, 8, 256)
    up, down, share = barrier((up, down, share))
    pieces += [up, down]
    up, down = shift(up, "z", 1), shift(down, "z", -1)
    share = lax.all_to_all(share, "z", 1, 0)
    up, down, share = barrier((up, down, share))
    pieces += [up, down]
    up, down = shift(up[:half], "z", 1), shift(down[half:], "z", -1)
    acc, dsq, nsq, send = inner(pos, noise_full, pieces)
    up, down, acc, send = barrier((up, down, acc, send))
    oth = swap(send, "c", 1)
    dist, dist_t, send = distance(pos, noise_full, up, down, acc, dsq, nsq)
    oth_last = swap(send, "c", 1)
    pieces += [up, down]

    noise_cols = lax.all_gather(share, plane, axis=0)
    noise_cols = noise_cols.reshape(16, 2, 8, cols // 16, 256)
    dist_all = lax.all_gather(dist_t, "z", axis=0)
    oth, oth_last, other = barrier((oth, oth_last, swap(dist, "c", 1)))
    dist = jnp.concatenate([dist, other], axis=1)

    both_rows = 2 * rows
    data_pot = jnp.zeros((both_rows,), F32)
    noise_pot = jnp.zeros((cols,), F32)
    for sweep in range(ITERS):
        scores = (data_pot[None, :] - dist) / EPSILON
        if sweep == 0:
            top = jnp.max(scores, axis=1)
            total = jnp.sum(jnp.exp(scores - top[:, None]), axis=1)
            top, total = row_total(jnp.stack([top, total]), merge)
        else:
            top = log_noise - noise_pot / EPSILON
            total = row_total(jnp.sum(jnp.exp(scores - top[:, None]), axis=1), add)
        noise_pot = EPSILON * log_noise - EPSILON * (top + jnp.log(total))
        scores = (noise_pot[:, None] - dist) / EPSILON
        if sweep == 0:
            top = jnp.max(scores, axis=0)
            total = jnp.sum(jnp.exp(scores - top[None, :]), axis=0)
            top, total = col_total(jnp.stack([top, total]), merge)
        else:
            top = log_data - data_pot / EPSILON
            total = jnp.sum(jnp.exp(scores - top[None, :]), axis=0)
            if sweep < ITERS - 1:
                total = col_total(total, add)
            else:
                both = [jnp.concatenate([total, noise_pot])]
                both += [swap(both[0], "z", k) for k in (1, 2, 3)]
                total = add([b[:both_rows] for b in both])
                both = jnp.concatenate([total] + [b[both_rows:] for b in both])
                far = swap(both, "z", 7)
                total = both[:both_rows] + far[:both_rows]
                pot_all = jnp.concatenate([both[both_rows:], far[both_rows:]])
        data_pot = EPSILON * log_data - EPSILON * (top + jnp.log(total))

    half = cols // 2
    norm = (log_noise - noise_pot / EPSILON)[:, None]
    up, low, *far = noise_part(pos, dist, data_pot[None, :], norm, pieces, oth, oth_last)
    up, low = up.reshape(4, 4, half + 8, 128), low.reshape(4, 4, half + 8, 128)
    up_far, low_far = scatter_far(up, far[:2], "x"), scatter_far(low, far[2:], "y")
    norm = (log_data - data_pot[:rows] / EPSILON)[:, None]
    data_target = data_target_of(
        pos, dist_all, pot_all.reshape(8, 1, cols), norm, noise_cols
    )
    near = [shift(up_far[0], "x", 1), shift(up_far[1], "x", -1)]
    near += [shift(low_far[0], "y", 1), shift(low_far[1], "y", -1)]
    near, data_target = barrier((near, data_target))
    up, low = up[0] + near[0] + near[1], low[0] + near[2] + near[3]
    up = up[0] + sum(shift(up[k], "y", k) for k in (1, 2, 3))
    low = low[0] + sum(shift(low[k], "x", k) for k in (1, 2, 3))
    noise_target = jnp.concatenate(
        [v[:half] / v[half : half + half // 128].reshape(half, 1) for v in (up, low)]
    )
    return (noise_target, data_target)


def solution(mesh):
    devices = mesh.devices.reshape(8, 4, 4, 2)
    torus = Mesh(devices, ("z", "y", "x", "c"))
    plane = ("y", "x", "c")
    return jax.shard_map(
        on_device,
        mesh=torus,
        in_specs=(P("z", plane), P(plane, "z")),
        out_specs=(P("z", plane), P(plane, "z")),
        check_vma=False,
    )
```

```python
import functools
import math

import jax
import jax.numpy as jnp
from jax import lax
from jax.experimental import pallas as pl
from jax.experimental.pallas import tpu as pltpu
from jax.sharding import Mesh, PartitionSpec as P

ITERS = 3
EPSILON = 0.02
BF16 = jnp.bfloat16
F32 = jnp.float32


def shift(v, axis, k):
    n = lax.axis_size(axis)
    return lax.ppermute(v, axis, [(i, (i + k) % n) for i in range(n)])


def swap(v, axis, k):
    n = lax.axis_size(axis)
    return lax.ppermute(v, axis, [(i, i ^ k) for i in range(n)])


def split(v):
    hi = v.astype(BF16)
    return hi, (v - hi.astype(F32)).astype(BF16)


def anywhere():
    return pl.BlockSpec(memory_space=pl.ANY)


def in_vmem():
    return pl.BlockSpec(memory_space=pltpu.VMEM)


def in_smem():
    return pl.BlockSpec(memory_space=pltpu.SMEM)


def params(mib):
    return pltpu.CompilerParams(vmem_limit_bytes=mib * 2**20)


def dot3(a, b, a_dim, b_dim):
    ah, al = split(a)
    bh, bl = split(b)
    return lax.dot_general(
        jnp.concatenate([ah, ah, al], axis=a_dim),
        jnp.concatenate([bh, bl, bh], axis=b_dim),
        (((a_dim,), (b_dim,)), ((), ())),
        preferred_element_type=F32,
    )


def lane_sums(v):
    return v[:, :128] + v[:, 128:256] + v[:, 256:384] + v[:, 384:]


def each(count, step):
    lax.fori_loop(0, count, lambda k, _: (step(k), 0)[1], 0)


OFFSETS = (0, 7, 1, 6, 2, 5, 3, 4)


def chunk_of(z, k):
    m = (k + 1) // 2
    return lax.rem(z + m + (k % 2) * (8 - 2 * m), 8)


def columns(z):
    return pl.ds(pl.multiple_of(z * 512, 512), 512)


def inner_kernel(pos, noise, *refs):
    pieces = refs[:7]
    acc, dsq, nsq, send, dacc, nacc, nbuf, dbuf, nsem, dsem, ssem = refs[7:]

    def fetch_noise(k):
        return pltpu.make_async_copy(
            noise.at[:, columns(chunk_of(pos[3], k))], nbuf.at[k], nsem.at[k]
        )

    def fetch_data(k, ref):
        return pltpu.make_async_copy(ref, dbuf.at[k], dsem.at[k])

    for k, ref in enumerate(pieces):
        fetch_noise(k).start()
        fetch_data(k, ref).start()
    fetch_noise(7).start()
    acc[...] = jnp.zeros_like(acc)
    dacc[...] = jnp.zeros_like(dacc)
    nacc[...] = jnp.zeros_like(nacc)

    def hand_on(k, j):
        lanes = pl.ds(pl.multiple_of(j * 256 + (1 - pos[0]) * 128, 128), 128)
        return pltpu.make_async_copy(
            dbuf.at[k, :, lanes], send.at[k, :, pl.ds(j * 128, 128)], ssem.at[k, j]
        )

    def step(k):
        fetch_noise(k).wait()
        fetch_data(k, pieces[0]).wait()
        for j in range(2):
            hand_on(k, j).start()
        n, d = nbuf[k], dbuf[k]
        acc[...] += dot3(n, d, 1, 1)
        dacc[...] += lane_sums(d * d)
        nacc[...] += lane_sums(n * n)

    each(7, step)
    fetch_noise(7).wait()
    n = nbuf[7]
    nsq[...] = jnp.sum(nacc[...] + lane_sums(n * n), axis=1, keepdims=True)
    dsq[...] = jnp.sum(dacc[...].T, axis=0, keepdims=True)

    def finish(k):
        for j in range(2):
            hand_on(k, j).wait()

    each(7, finish)


def inner(pos, noise, pieces):
    cols, rows = noise.shape[0], pieces[0].shape[0]
    return pl.pallas_call(
        inner_kernel,
        in_specs=[in_smem()] + [anywhere()] * 8,
        out_specs=[in_vmem()] * 3 + [anywhere()],
        out_shape=[
            jax.ShapeDtypeStruct((cols, rows), F32),
            jax.ShapeDtypeStruct((1, rows), F32),
            jax.ShapeDtypeStruct((cols, 1), F32),
            jax.ShapeDtypeStruct((7, rows, 256), F32),
        ],
        scratch_shapes=[
            pltpu.VMEM((rows, 128), F32),
            pltpu.VMEM((cols, 128), F32),
            pltpu.VMEM((8, cols, 512), F32),
            pltpu.VMEM((7, rows, 512), F32),
            pltpu.SemaphoreType.DMA((8,)),
            pltpu.SemaphoreType.DMA((7,)),
            pltpu.SemaphoreType.DMA((7, 2)),
        ],
        compiler_params=params(56),
        cost_estimate=pl.CostEstimate(
            flops=6 * cols * rows * 3584, bytes_accessed=15 * 2**20, transcendentals=0
        ),
        name="inner_products",
    )(pos, noise, *pieces)


def distance_kernel(pos, dsq, *refs):
    sources, outs, held, sems = refs[:5], refs[5:8], refs[8:13], refs[13]
    sources = (sources[0].at[:, columns(lax.rem(pos[3] + 4, 8))],) + sources[1:]
    dist, dist_t, send = outs
    copies = [
        pltpu.make_async_copy(source, at, sems.at[k])
        for k, (source, at) in enumerate(zip(sources, held))
    ]
    for copy in copies:
        copy.start()
    for copy in copies:
        copy.wait()
    noise, top, low, acc, nsq = held
    d = jnp.concatenate([top[...], low[...]], axis=0)
    inner_prod = acc[...] + dot3(noise[...], d, 1, 1)
    data_sq = dsq[...] + jnp.sum(lane_sums(d * d).T, axis=0, keepdims=True)
    res = (nsq[...] + data_sq - 2.0 * inner_prod) * (1.0 / 4096)
    dist[...] = res
    dist_t[...] = res.T
    for j in range(2):
        first = d[:, j * 256 : j * 256 + 128]
        second = d[:, j * 256 + 128 : j * 256 + 256]
        send[:, j * 128 : (j + 1) * 128] = jnp.where(pos[0] == 0, second, first)


def distance(pos, noise, top, low, acc, dsq, nsq):
    cols, rows = acc.shape
    return pl.pallas_call(
        distance_kernel,
        in_specs=[in_smem(), in_vmem()] + [anywhere()] * 5,
        out_specs=[in_vmem()] * 3,
        out_shape=[
            jax.ShapeDtypeStruct((cols, rows), F32),
            jax.ShapeDtypeStruct((rows, cols), F32),
            jax.ShapeDtypeStruct((rows, 256), F32),
        ],
        scratch_shapes=[
            pltpu.VMEM((cols, 512), F32),
            pltpu.VMEM((rows // 2, 512), F32),
            pltpu.VMEM((rows // 2, 512), F32),
            pltpu.VMEM((cols, rows), F32),
            pltpu.VMEM((cols, 1), F32),
            pltpu.SemaphoreType.DMA((5,)),
        ],
        compiler_params=params(56),
        cost_estimate=pl.CostEstimate(
            flops=6 * cols * rows * 512, bytes_accessed=4 * 2**20, transcendentals=0
        ),
        name="distance",
    )(pos, dsq, noise, top, low, acc, nsq)


def noise_part_kernel(pos, dist, pot, norm, *refs):
    pieces, oth, oth_last = refs[:9], refs[9], refs[10]
    up, low, far, refs = refs[11], refs[12], refs[13:17], refs[17:]
    wcat, dbuf, obuf, sums, dsem, osem, ssem, fsem = refs
    core, x, y, z = pos[0], pos[1], pos[2], pos[3]
    rows, depth = dist.shape
    half, mine = rows // 2, depth // 2
    part = mine // 2

    def fetch(k, ref, first, sem):
        copies = []
        for j in range(2):
            lanes = pl.ds(pl.multiple_of(j * 256 + core * 128, 128), 128)
            at = dbuf.at[k, pl.ds(first, ref.shape[0]), pl.ds(j * 128, 128)]
            copies.append(pltpu.make_async_copy(ref.at[:, lanes], at, dsem.at[k, sem + j]))
        return copies

    def fetch_other(k, ref):
        return pltpu.make_async_copy(ref, dbuf.at[k, pl.ds(mine, mine)], dsem.at[k, 4])

    last = fetch(7, pieces[7], 0, 0) + fetch(7, pieces[8], part, 2)
    last.append(fetch_other(7, oth_last))
    for k in range(7):
        for copy in fetch(k, pieces[k], 0, 0):
            copy.start()
        fetch_other(k, oth.at[k]).start()
    for copy in last:
        copy.start()
    h, l = split(jnp.exp((pot[...] - dist[...]) / EPSILON - norm[...]))
    wcat[:, :depth] = h
    wcat[:, depth : 2 * depth] = h
    wcat[:, 2 * depth :] = l
    total = lax.dot_general(
        jnp.ones((16, 2 * depth), BF16),
        wcat[:, depth:],
        (((1,), (1,)), ((), ())),
        preferred_element_type=F32,
    )
    for k in range(2):
        for j in range(half // 128):
            first = k * half + j * 128
            sums[k, j : j + 1, :] = total[:1, first : first + 128]
        sums[k, half // 128 :, :] = jnp.zeros((8 - half // 128, 128), F32)

    def place(g, k, ref, slot, sem):
        return (
            pltpu.make_async_copy(
                obuf.at[g, pl.ds(k * half, half)], ref.at[slot, pl.ds(0, half)], sem[0]
            ),
            pltpu.make_async_copy(
                sums.at[k], ref.at[slot, pl.ds(half, 8)], sem[1]
            ),
        )

    def stores(g, act):
        dy = lax.rem(g // 4 - y + 4, 4)
        dx = lax.rem(lax.rem(g, 4) - x + 4, 4)
        for k, (ref, major, minor) in enumerate(((up, dx, dy), (low, dy, dx))):
            sem = (osem.at[k, g], ssem.at[k, g])
            for copy in place(g, k, ref, major * 4 + minor, sem):
                act(copy)
            for j in range(2):
                sem = (fsem.at[k, minor, 0], fsem.at[k, minor, 1])

                @pl.when((major == 2) & (minor // 2 == j))
                def _():
                    slot = lax.rem(minor, 2)
                    for copy in place(g, k, far[2 * k + j], slot, sem):
                        act(copy)

    def step(k):
        h, l = split(dbuf[k])
        res = lax.dot_general(
            wcat[...],
            jnp.concatenate([h, l, h], axis=0),
            (((1,), (0,)), ((), ())),
            preferred_element_type=F32,
        )
        for j in range(2):
            g = 2 * chunk_of(z, k) + j
            obuf[g] = res[:, j * 128 : (j + 1) * 128]
            stores(g, lambda copy: copy.start())

    def fetched(k):
        for copy in fetch(k, pieces[0], 0, 0):
            copy.wait()
        fetch_other(k, oth_last).wait()
        step(k)

    each(7, fetched)
    for copy in last:
        copy.wait()
    step(7)

    each(16, lambda g: stores(g, lambda copy: copy.wait()))


def noise_part(pos, dist, pot, norm, pieces, oth, oth_last):
    rows, depth = dist.shape
    return pl.pallas_call(
        noise_part_kernel,
        in_specs=[in_smem()] + [in_vmem()] * 3 + [anywhere()] * 11,
        out_specs=[anywhere()] * 6,
        out_shape=[jax.ShapeDtypeStruct((16, rows // 2 + 8, 128), F32)] * 2
        + [jax.ShapeDtypeStruct((2, rows // 2 + 8, 128), F32)] * 4,
        scratch_shapes=[
            pltpu.VMEM((rows, 3 * depth), BF16),
            pltpu.VMEM((8, depth, 256), F32),
            pltpu.VMEM((16, rows, 128), F32),
            pltpu.VMEM((2, 8, 128), F32),
            pltpu.SemaphoreType.DMA((8, 5)),
            pltpu.SemaphoreType.DMA((2, 16)),
            pltpu.SemaphoreType.DMA((2, 16)),
            pltpu.SemaphoreType.DMA((2, 4, 2)),
        ],
        compiler_params=params(56),
        cost_estimate=pl.CostEstimate(
            flops=6 * rows * depth * 2048, bytes_accessed=12 * 2**20, transcendentals=0
        ),
        name="noise_part",
    )(pos, dist, pot, norm, *pieces, oth, oth_last)


def slot_of(k):
    return jnp.where(k < 4, k, 11 - k)


def data_target_kernel(pos, dist, pot, norm, noise, out, dbuf, nbuf, dsem, nsem):
    def fetch(k):
        copies = [pltpu.make_async_copy(dist.at[k], dbuf.at[k], dsem.at[k])]
        for c in range(2):
            for j in range(2):
                lanes = pl.ds(j * 256 + c * 128, 128)
                copies.append(
                    pltpu.make_async_copy(
                        noise.at[:, c, k, :, pl.ds(j * 128, 128)],
                        nbuf.at[k, :, :, lanes],
                        nsem.at[k, 2 * c + j],
                    )
                )
        return copies

    def start(k):
        for copy in fetch(k):
            copy.start()

    each(8, start)
    out[...] = jnp.zeros_like(out)

    def step(k):
        for copy in fetch(k):
            copy.wait()
        own = pot[slot_of(jnp.bitwise_xor(k, pos[3]))]
        w = jnp.exp((own - dbuf[k]) / EPSILON - norm[...])
        n = nbuf[k]
        out[...] += dot3(w, n.reshape(n.shape[0] * n.shape[1], n.shape[2]), 1, 0)

    each(8, step)


def data_target_of(pos, dist, pot, norm, noise):
    _, rows, depth = dist.shape
    shares, _, _, share, _ = noise.shape
    width = 512
    return pl.pallas_call(
        data_target_kernel,
        in_specs=[in_smem(), anywhere(), in_vmem(), in_vmem(), anywhere()],
        out_specs=in_vmem(),
        out_shape=jax.ShapeDtypeStruct((rows, width), F32),
        scratch_shapes=[
            pltpu.VMEM((8, rows, depth), F32),
            pltpu.VMEM((8, shares, share, width), F32),
            pltpu.SemaphoreType.DMA((8,)),
            pltpu.SemaphoreType.DMA((8, 4)),
        ],
        compiler_params=params(56),
        cost_estimate=pl.CostEstimate(
            flops=6 * rows * depth * 8 * width,
            bytes_accessed=15 * 2**20,
            transcendentals=8 * rows * depth,
        ),
        name="data_target",
    )(pos, dist, pot, norm, noise)


def others(v, axis):
    return [swap(v, axis, k) for k in (1, 2, 3)]


def merge(parts):
    top = functools.reduce(jnp.maximum, [p[0] for p in parts])
    total = sum(p[1] * jnp.exp(p[0] - top) for p in parts)
    return jnp.stack([top, total])


def add(parts):
    return sum(parts)


def row_total(v, join):
    v = join([v] + others(v, "x"))
    return join([v] + others(v, "y"))


def col_total(v, join):
    v = join([v] + [swap(v, "z", k) for k in (1, 2, 3)])
    return join([v, swap(v, "z", 7)])


def scatter_far(chunks, far, axis):
    n = far[0].shape[0]
    up, down = shift(far[0], axis, 1), shift(far[1], axis, -1)
    up = jnp.concatenate([chunks[1][:n] + up, chunks[1][n:]])
    down = jnp.concatenate([chunks[3][:n], chunks[3][n:] + down])
    return up, down


def on_device(noise, data):
    cols, rows = noise.shape[0], data.shape[0]
    log_noise = -math.log(cols * lax.axis_size("z"))
    log_data = -math.log(rows * 32)
    pos = jnp.stack([lax.axis_index(a).astype(jnp.int32) for a in ("c", "x", "y", "z")])
    barrier = lax.optimization_barrier
    plane = ("y", "x", "c")

    noise_full = lax.all_gather(noise, plane, axis=1, tiled=True)
    half = rows // 2
    up, down = shift(data, "z", 1), shift(data, "z", -1)
    share = lax.all_to_all(noise.reshape(4, 4, cols // 16, 128), "x", 1, 2)
    up, down, share = barrier((up, down, share))
    pieces = [data, up, down]
    up, down = shift(up, "z", 1), shift(down, "z", -1)
    share = lax.all_to_all(share, "y", 0, 1).reshape(cols // 16, 8, 256)
    up, down, share = barrier((up, down, share))
    pieces += [up, down]
    up, down = shift(up, "z", 1), shift(down, "z", -1)
    share = lax.all_to_all(share, "z", 1, 0)
    up, down, share = barrier((up, down, share))
    pieces += [up, down]
    up, down = shift(up[:half], "z", 1), shift(down[half:], "z", -1)
    acc, dsq, nsq, send = inner(pos, noise_full, pieces)
    up, down, acc, send = barrier((up, down, acc, send))
    oth = swap(send, "c", 1)
    dist, dist_t, send = distance(pos, noise_full, up, down, acc, dsq, nsq)
    oth_last = swap(send, "c", 1)
    pieces += [up, down]

    noise_cols = lax.all_gather(share, plane, axis=0)
    noise_cols = noise_cols.reshape(16, 2, 8, cols // 16, 256)
    dist_all = lax.all_gather(dist_t, "z", axis=0)
    oth, oth_last, other = barrier((oth, oth_last, swap(dist, "c", 1)))
    dist = jnp.concatenate([dist, other], axis=1)

    both_rows = 2 * rows
    data_pot = jnp.zeros((both_rows,), F32)
    noise_pot = jnp.zeros((cols,), F32)
    for sweep in range(ITERS):
        scores = (data_pot[None, :] - dist) / EPSILON
        if sweep == 0:
            top = jnp.max(scores, axis=1)
            total = jnp.sum(jnp.exp(scores - top[:, None]), axis=1)
            top, total = row_total(jnp.stack([top, total]), merge)
        else:
            top = log_noise - noise_pot / EPSILON
            total = row_total(jnp.sum(jnp.exp(scores - top[:, None]), axis=1), add)
        noise_pot = EPSILON * log_noise - EPSILON * (top + jnp.log(total))
        scores = (noise_pot[:, None] - dist) / EPSILON
        if sweep == 0:
            top = jnp.max(scores, axis=0)
            total = jnp.sum(jnp.exp(scores - top[None, :]), axis=0)
            top, total = col_total(jnp.stack([top, total]), merge)
        else:
            top = log_data - data_pot / EPSILON
            total = jnp.sum(jnp.exp(scores - top[None, :]), axis=0)
            if sweep < ITERS - 1:
                total = col_total(total, add)
            else:
                both = [jnp.concatenate([total, noise_pot])]
                both += [swap(both[0], "z", k) for k in (1, 2, 3)]
                total = add([b[:both_rows] for b in both])
                both = jnp.concatenate([total] + [b[both_rows:] for b in both])
                far = swap(both, "z", 7)
                total = both[:both_rows] + far[:both_rows]
                pot_all = jnp.concatenate([both[both_rows:], far[both_rows:]])
        data_pot = EPSILON * log_data - EPSILON * (top + jnp.log(total))

    half = cols // 2
    norm = (log_noise - noise_pot / EPSILON)[:, None]
    up, low, *far = noise_part(pos, dist, data_pot[None, :], norm, pieces, oth, oth_last)
    up, low = up.reshape(4, 4, half + 8, 128), low.reshape(4, 4, half + 8, 128)
    up_far, low_far = scatter_far(up, far[:2], "x"), scatter_far(low, far[2:], "y")
    norm = (log_data - data_pot[:rows] / EPSILON)[:, None]
    data_target = data_target_of(
        pos, dist_all, pot_all.reshape(8, 1, cols), norm, noise_cols
    )
    near = [shift(up_far[0], "x", 1), shift(up_far[1], "x", -1)]
    near += [shift(low_far[0], "y", 1), shift(low_far[1], "y", -1)]
    near, data_target = barrier((near, data_target))
    up, low = up[0] + near[0] + near[1], low[0] + near[2] + near[3]
    up = up[0] + sum(shift(up[k], "y", k) for k in (1, 2, 3))
    low = low[0] + sum(shift(low[k], "x", k) for k in (1, 2, 3))
    noise_target = jnp.concatenate(
        [v[:half] / v[half : half + half // 128].reshape(half, 1) for v in (up, low)]
    )
    return (noise_target, data_target)


def solution(mesh):
    devices = mesh.devices.reshape(8, 4, 4, 2)
    torus = Mesh(devices, ("z", "y", "x", "c"))
    plane = ("y", "x", "c")
    return jax.shard_map(
        on_device,
        mesh=torus,
        in_specs=(P("z", plane), P(plane, "z")),
        out_specs=(P("z", plane), P(plane, "z")),
        check_vma=False,
    )
```
